32 devices in a mesh: term: 8 (over z, core), row: 4 (over y, x).
Axes of the slice: x: 2, y: 2, z: 4, core: 2. Of those that a mesh axis runs over, the one named last changes fastest.
Arguments:
- psi: bfloat16 [2048, 2048], P('row'), may hold values from -6 to 6
- left_ops: bfloat16 [8, 2048, 2048], P('term', 'row'), may hold values from -0.046875 to 0.046875
- right_ops: bfloat16 [8, 2048, 2048], P('term', 'row'), may hold values from -0.1875 to 0.1875
- block_mask: int32 [8, 16, 16], P('term', 'row'), may hold values from 0 to 1, as said below
Outputs:
- sigma: bfloat16 [2048, 2048], P('row', 'term')
The draws below stay inside these ranges and needn't reach their ends.
Inputs may be any that keep to these rules, and one draw needn't show every extreme that they name: Entries are 0 or 1; block_mask[t, i, i] = 1 for every term and block.
All inputs are finite; a program needn't handle non-finite values.
Results may differ from the reference program's by a relative error of at most 0.0049.
Values may be sent and summed in bfloat16 or wider, within the bound.
No kernel may reach another device: no remote copies, remote signals or barrier semaphores. Data moves between devices by JAX's collectives and lax.ppermute only.
A program may use at most 64 MiB of HBM per device.

```python
import jax
import jax.numpy as jnp
from jax import lax

S = 2048
BLK = 128
NB = 16
TERMS = 8


def draw_block_mask(key, part):
    first, second = jax.random.split(jax.random.fold_in(key, 7))
    level = jax.random.randint(first, (TERMS, 1, 1), 1, 9)
    coins = jax.random.randint(second, (TERMS, NB, NB), 0, 8)
    diagonal = jnp.eye(NB, dtype=jnp.int32)
    return jnp.maximum((coins < level).astype(jnp.int32), diagonal[None])


def raised(drawn, key, source, target, shards_of, factor):
    def block_of(position):
        return (jnp.arange(drawn.shape[position]) // (drawn.shape[position] // shards_of)).reshape((-1,) + (1,) * (drawn.ndim - 1 - position))

    near = jax.random.permutation(key, shards_of)[block_of(target)]
    second = (block_of(target) + shards_of // 2) % shards_of
    return jnp.where((block_of(source) == near) | (block_of(source) == second), factor * drawn, drawn)


def steps_of(key, shape, cuts, least, high):
    factor_of = 1.0
    for axis_at, blocks in cuts:
        heights = jax.random.uniform(jax.random.fold_in(jax.random.fold_in(key, 6), axis_at), (blocks,), jnp.float32, least / len(cuts), high / len(cuts))
        factor_of = factor_of * jnp.repeat(jnp.exp(heights), shape[axis_at] // blocks).reshape((-1,) + (1,) * (len(shape) - 1 - axis_at))
    return factor_of


def bell_draw(key, shape, deviation, bound, cuts=(), kind=jnp.bfloat16):
    entries = deviation * jax.random.normal(key, shape, jnp.float32)
    if cuts:
        entries = entries * steps_of(key, shape, cuts, -0.22, 0.18)
    return jnp.clip(entries, -bound, bound).astype(kind)


def bell_draw_with(rng, shape, width, reach, pieces, heavy, held_as=jnp.bfloat16):
    array = width * jax.random.normal(rng, shape, jnp.float32)
    if pieces:
        array = array * steps_of(rng, shape, pieces, -0.22, 0.18)
    return jnp.clip(raised(array, jax.random.fold_in(rng, 3), *heavy), -reach, reach).astype(held_as)


def setup_inputs(seed: int = 0) -> dict:
    streams_of = jax.random.split(jax.random.key(seed), 5)
    return {
        "psi": bell_draw(streams_of[0], (S, S), 1.0, 6.0, ((0, 4),)),
        "left_ops": bell_draw(streams_of[1], (TERMS, S, S), (S * TERMS) ** -0.5, 0.046875, ((0, 8), (1, 4))),
        "right_ops": bell_draw_with(streams_of[2], (TERMS, S, S), S ** -0.5, 0.1875, ((0, 8), (1, 4)), (0, 1, 8, 2.0)),
        "block_mask": draw_block_mask(jax.random.fold_in(streams_of[4], 71), 0),
    }


def expand_mask(mask):
    blocks = mask.shape[0]
    grid = jnp.broadcast_to(mask[:, None, :, None], (blocks, BLK, blocks, BLK))
    return grid.reshape(blocks * BLK, blocks * BLK)


def reference(psi, left_ops, right_ops, block_mask):
    psi_wide = psi.astype(jnp.float32)

    def one_term(total, items):
        left, right, mask = items
        masked = left * expand_mask(mask).astype(jnp.bfloat16)
        inner = jnp.dot(masked.astype(jnp.float32), psi_wide).astype(jnp.bfloat16)
        total = total + jnp.dot(inner.astype(jnp.float32), right.astype(jnp.float32).T)
        return total, None

    start = jnp.zeros((S, S), jnp.float32)
    total, unused = lax.scan(one_term, start, (left_ops, right_ops, block_mask))
    return total.astype(jnp.bfloat16)
```

```python
import functools
import math

import jax
import jax.numpy as jnp
from jax import lax
from jax.experimental import pallas as pl
from jax.experimental.pallas import tpu as pltpu
from jax.sharding import PartitionSpec as P

SHARE = 4
PIECES = 2
VMEM_BYTES = 48 * 1024 * 1024
WHOLE = pl.BlockSpec(memory_space=pltpu.VMEM)
ANYWHERE = pl.BlockSpec(memory_space=pl.ANY)


def params():
    return pltpu.CompilerParams(vmem_limit_bytes=VMEM_BYTES)


def mask_kernel(start, blk, mask_ref, left_ref, out_ref):
    block = (start + pl.program_id(0) * left_ref.shape[0]) // blk
    for j in range(left_ref.shape[1] // blk):
        keep = mask_ref[block, j] != 0
        cols = pl.ds(j * blk, blk)
        tile = left_ref[:, cols]
        out_ref[:, cols] = jnp.where(keep, tile, jnp.zeros_like(tile))


def masked_rows(left, mask, start, rows):
    width = left.shape[1]
    blk = width // mask.shape[1]
    unit = math.gcd(rows, blk)
    return pl.pallas_call(
        functools.partial(mask_kernel, start, blk),
        grid=(rows // unit,),
        in_specs=[
            pl.BlockSpec(memory_space=pltpu.SMEM),
            pl.BlockSpec((unit, width), lambda i: (start // unit + i, 0)),
        ],
        out_specs=pl.BlockSpec((unit, width), lambda i: (i, 0)),
        out_shape=jax.ShapeDtypeStruct((rows, width), left.dtype),
        compiler_params=params(),
        cost_estimate=pl.CostEstimate(
            flops=rows * width, bytes_accessed=4 * rows * width, transcendentals=0
        ),
    )(mask, left)


def inner_kernel(n_rows, n_parts, place_ref, *refs):
    row_refs = refs[:n_rows]
    part_refs = refs[n_rows : n_rows + n_parts]
    out_ref, psi, sems = refs[n_rows + n_parts :]
    copies = []
    for p, part in enumerate(part_refs):
        size = part.shape[0]
        where = pl.ds(pl.multiple_of(place_ref[p], size), size)
        copies.append(pltpu.make_async_copy(part, psi.at[where], sems.at[p]))
    for copy in copies:
        copy.start()
    for copy in copies:
        copy.wait()
    width = psi.shape[1]
    step = math.gcd(width, 512)

    def column(j, carry):
        cols = pl.ds(pl.multiple_of(j * step, step), step)
        at = 0
        for ref in row_refs:
            unit = math.gcd(ref.shape[0], 256)
            for i in range(ref.shape[0] // unit):
                value = jnp.dot(
                    ref[i * unit : (i + 1) * unit, :],
                    psi[:, cols],
                    preferred_element_type=jnp.float32,
                )
                out_ref[at : at + unit, cols] = value.astype(out_ref.dtype)
                at += unit
        return carry

    lax.fori_loop(0, width // step, column, 0)


def inner_of(rows, parts, places):
    height = sum(a.shape[0] for a in rows)
    width = parts[0].shape[1]
    depth = sum(a.shape[0] for a in parts)
    return pl.pallas_call(
        functools.partial(inner_kernel, len(rows), len(parts)),
        in_specs=[pl.BlockSpec(memory_space=pltpu.SMEM)]
        + [WHOLE] * len(rows)
        + [ANYWHERE] * len(parts),
        out_specs=WHOLE,
        out_shape=jax.ShapeDtypeStruct((height, width), parts[0].dtype),
        scratch_shapes=[
            pltpu.VMEM((depth, width), parts[0].dtype),
            pltpu.SemaphoreType.DMA((len(parts),)),
        ],
        compiler_params=params(),
        cost_estimate=pl.CostEstimate(
            flops=2 * height * width * depth,
            bytes_accessed=2 * (height * depth + height * width + width * depth),
            transcendentals=0,
        ),
    )(places, *rows, *parts)


def outer_kernel(n_inner, n_right, side_ref, *refs):
    inner_refs = refs[:n_inner]
    right_refs = refs[n_inner : n_inner + n_right]
    keep_ref, give_ref = refs[n_inner + n_right :]
    side = side_ref[0]
    for half, out_ref in ((side, keep_ref), (1 - side, give_ref)):
        right = jnp.concatenate([ref[half] for ref in right_refs], 0)
        at = 0
        for ref in inner_refs:
            unit = math.gcd(ref.shape[0], 256)
            for i in range(ref.shape[0] // unit):
                out_ref[at : at + unit, :] = lax.dot_general(
                    ref[i * unit : (i + 1) * unit, :],
                    right,
                    (((1,), (1,)), ((), ())),
                    preferred_element_type=jnp.float32,
                )
                at += unit


def outer_of(inners, own_right, piece, rights, side):
    height = sum(a.shape[0] for a in inners)
    halves, pieces, wide, depth = own_right.shape
    width = wide * (1 + len(rights))
    shape = jax.ShapeDtypeStruct((height, width), jnp.float32)
    own_spec = pl.BlockSpec((halves, None, wide, depth), lambda i: (0, piece, 0, 0))
    return pl.pallas_call(
        functools.partial(outer_kernel, len(inners), 1 + len(rights)),
        grid=(1,),
        in_specs=[pl.BlockSpec(memory_space=pltpu.SMEM)]
        + [WHOLE] * len(inners)
        + [own_spec]
        + [WHOLE] * len(rights),
        out_specs=[WHOLE, WHOLE],
        out_shape=[shape, shape],
        compiler_params=params(),
        cost_estimate=pl.CostEstimate(
            flops=4 * height * width * depth,
            bytes_accessed=2 * depth * (height + 2 * width) + 8 * height * width,
            transcendentals=0,
        ),
    )(side, *inners, own_right, *rights)


def after(value, *earlier):
    return lax.optimization_barrier((value, *earlier))[0]


def pick(value, index, axis):
    return lax.dynamic_index_in_dim(value, index, axis, keepdims=False)


def shards(psi, left_ops, right_ops, block_mask):
    terms, n = lax.axis_size("term"), lax.axis_size("row")
    s = math.isqrt(n)
    assert s * s == n and terms == 2 * n and left_ops.shape[0] == 1
    height, width = psi.shape
    term, row = lax.axis_index("term"), lax.axis_index("row")
    core, z = term % 2, term // 2
    zh, zl = z // s, z % s
    hi, lo = row // s, row % s

    def from_lo(value, j):
        pairs = [(a * s + (b + j) % s, a * s + b) for a in range(s) for b in range(s)]
        return lax.ppermute(value, "row", pairs)

    def from_hi(value, j):
        pairs = [(((a + j) % s) * s + b, a * s + b) for a in range(s) for b in range(s)]
        return lax.ppermute(value, "row", pairs)

    def from_term(value, bit):
        return lax.ppermute(value, "term", [(a ^ bit, a) for a in range(terms)])

    def to_zl(value, j):
        pairs = [
            ((a * s + b) * 2 + c, (a * s + (b + j) % s) * 2 + c)
            for a in range(s) for b in range(s) for c in range(2)
        ]
        return lax.ppermute(value, "term", pairs)

    def to_zh(value, j):
        pairs = [
            ((a * s + b) * 2 + c, (((a + j) % s) * s + b) * 2 + c)
            for a in range(s) for b in range(s) for c in range(2)
        ]
        return lax.ppermute(value, "term", pairs)

    def crossed(value):
        pairs = [
            (((a * s + b) * 2 + c) * n + y * s + x, ((a * s + x) * 2 + c) * n + y * s + b)
            for a in range(s) for b in range(s) for c in range(2) for y in range(s) for x in range(s)
        ]
        return lax.ppermute(value, ("term", "row"), pairs)

    share = height // SHARE
    mine = term % SHARE
    own_share = lax.dynamic_slice_in_dim(psi, mine * share, share, 0)
    fetched = {(0, 0): own_share}
    for jx in range(1, s):
        fetched[0, jx] = from_lo(own_share, jx)
    for jx in range(s):
        for jy in range(1, s):
            fetched[jy, jx] = from_hi(fetched[0, jx], jy)
    parts, places = [psi], [row * height]
    for (jy, jx), value in fetched.items():
        if (jy, jx) == (0, 0):
            continue
        block = (hi + jy) % s * s + (lo + jx) % s
        along = from_term(value, 2)
        for bits, part in ((0, value), (1, from_term(value, 1)), (2, along), (3, from_term(along, 1))):
            parts.append(part)
            places.append(block * height + (mine ^ bits) * share)
    places = jnp.stack(places).astype(jnp.int32)

    left, mask = left_ops[0], block_mask[0]
    size = height // PIECES
    own_left = [masked_rows(left, mask, p * size, size) for p in range(PIECES)]
    earlier = [fetched[0, jx] for jx in range(1, s)]
    near_left = []
    for p in range(PIECES):
        got = [from_lo(after(own_left[p], *earlier), j) for j in range(1, s)]
        near_left.append(got)
        earlier = got

    wide = height // (2 * PIECES)
    own_right = right_ops[0].reshape(2, PIECES, wide, width)
    earlier = [fetched[jy, jx] for jy in range(1, s) for jx in range(s)]
    near_right = []
    for p in range(PIECES):
        got = [from_hi(after(own_right[:, p], *earlier), j) for j in range(1, s)]
        near_right.append(got)
        earlier = got

    inners = [inner_of(own_left, parts, places)]
    for j in range(s - 1):
        for p in range(PIECES):
            inners.append(inner_of([near_left[p][j]], parts, places))

    side = core.astype(jnp.int32).reshape(1)
    outs = []
    for p in range(PIECES):
        keep, give = outer_of(inners, own_right, p, near_right[p], side)
        total = (keep + from_term(give, 1)).reshape(s, height, s, wide)
        kept = pick(total, (zl - lo) % s, 0)
        for j in range(1, s):
            sent = pick(total, (zl + j - lo) % s, 0).astype(jnp.bfloat16)
            kept = kept + to_zl(sent, j).astype(jnp.float32)
        final = pick(kept, (zh - hi) % s, 1)
        for j in range(1, s):
            sent = pick(kept, (zh + j - hi) % s, 1).astype(jnp.bfloat16)
            final = final + to_zh(sent, j).astype(jnp.float32)
        outs.append(crossed(final.astype(jnp.bfloat16)))
    return jnp.concatenate(outs, 1)


def solution(mesh):
    in_specs = (
        P("row", None),
        P("term", "row", None),
        P("term", "row", None),
        P("term", "row", None),
    )
    out_specs = P("row", "term")
    return jax.shard_map(shards, mesh=mesh, in_specs=in_specs, out_specs=out_specs, check_vma=False)
```

```python
import functools
import math

import jax
import jax.numpy as jnp
from jax import lax
from jax.experimental import pallas as pl
from jax.experimental.pallas import tpu as pltpu
from jax.sharding import PartitionSpec as P

SHARE = 4
PIECES = 2
VMEM_BYTES = 20 * 1024 * 1024
COST = pl.CostEstimate(flops=1, bytes_accessed=1, transcendentals=0)
WHOLE = pl.BlockSpec(memory_space=pltpu.VMEM)
SCALARS = pl.BlockSpec(memory_space=pltpu.SMEM)
ANYWHERE = pl.BlockSpec(memory_space=pl.ANY)


def params():
    return pltpu.CompilerParams(vmem_limit_bytes=VMEM_BYTES)


def mask_kernel(blk, mask_ref, left_ref, out_ref):
    for j in range(left_ref.shape[1] // blk):
        keep = mask_ref[pl.program_id(0), j] != 0
        cols = pl.ds(j * blk, blk)
        tile = left_ref[:, cols]
        out_ref[:, cols] = jnp.where(keep, tile, jnp.zeros_like(tile))


def masked_rows(left, mask):
    rows, width = left.shape
    blk = width // mask.shape[1]
    spec = pl.BlockSpec((blk, width), lambda i: (i, 0))
    return pl.pallas_call(
        functools.partial(mask_kernel, blk),
        grid=(rows // blk,),
        in_specs=[SCALARS, spec],
        out_specs=spec,
        out_shape=jax.ShapeDtypeStruct((rows, width), left.dtype),
        compiler_params=params(),
        cost_estimate=COST,
    )(mask, left)


def stack_kernel(*refs):
    part_refs, (whole, sems) = refs[:-2], refs[-2:]
    copies, at = [], 0
    for p, part in enumerate(part_refs):
        size = part.shape[0]
        copies.append(pltpu.make_async_copy(part, whole.at[pl.ds(at, size)], sems.at[p]))
        at += size
    for copy in copies:
        copy.start()
    for copy in copies:
        copy.wait()


def stacked(parts):
    depth, width = sum(a.shape[0] for a in parts), parts[0].shape[1]
    return pl.pallas_call(
        stack_kernel,
        in_specs=[ANYWHERE] * len(parts),
        out_specs=ANYWHERE,
        out_shape=jax.ShapeDtypeStruct((depth, width), parts[0].dtype),
        scratch_shapes=[pltpu.SemaphoreType.DMA((len(parts),))],
        compiler_params=params(),
        cost_estimate=COST,
    )(*parts)


def inner_kernel(sizes, place_ref, rows_ref, *refs):
    part_refs, (out_ref, ordered) = refs[:-2], refs[-2:]

    @pl.when(pl.program_id(0) == 0)
    def _():
        at = 0
        for p, size in enumerate(sizes):
            cols = pl.ds(pl.multiple_of(place_ref[p], size), size)
            ordered[:, at : at + size] = rows_ref[:, cols]
            at += size

    psi = jnp.concatenate([ref[...] for ref in part_refs], 0)
    unit = math.gcd(rows_ref.shape[0], 256)
    for i in range(rows_ref.shape[0] // unit):
        rows = pl.ds(i * unit, unit)
        value = jnp.dot(ordered[rows, :], psi, preferred_element_type=jnp.float32)
        out_ref[rows, :] = value.astype(out_ref.dtype)


def inner_of(rows, parts, sizes, places):
    height, depth = rows.shape
    width = parts[0].shape[1]
    step = math.gcd(width, 512)
    return pl.pallas_call(
        functools.partial(inner_kernel, sizes),
        grid=(width // step,),
        in_specs=[SCALARS, pl.BlockSpec((height, depth), lambda j: (0, 0))]
        + [pl.BlockSpec((a.shape[0], step), lambda j: (0, j)) for a in parts],
        out_specs=pl.BlockSpec((height, step), lambda j: (0, j)),
        out_shape=jax.ShapeDtypeStruct((height, width), parts[0].dtype),
        scratch_shapes=[pltpu.VMEM((height, depth), rows.dtype)],
        compiler_params=params(),
        cost_estimate=COST,
    )(places, rows, *parts)


def outer_kernel(n_inner, n_right, side_ref, *refs):
    inner_refs = refs[:n_inner]
    right_refs = refs[n_inner : n_inner + n_right]
    keep_ref, give_ref = refs[n_inner + n_right :]
    side = side_ref[0]
    wide = keep_ref.shape[2]
    for half, out_ref in ((1 - side, give_ref), (side, keep_ref)):
        right = jnp.concatenate([ref[half] for ref in right_refs], 0)
        at = 0
        for ref in inner_refs:
            unit = math.gcd(ref.shape[0], 256)
            for i in range(ref.shape[0] // unit):
                value = lax.dot_general(
                    ref[i * unit : (i + 1) * unit, :],
                    right,
                    (((1,), (1,)), ((), ())),
                    preferred_element_type=jnp.float32,
                )
                for j in range(n_right):
                    out_ref[j, at : at + unit, :] = value[:, j * wide : (j + 1) * wide]
                at += unit


def outer_of(inners, piece, rights, side):
    height = sum(a.shape[0] for a in inners)
    halves, pieces, wide, depth = rights[0].shape
    n_right = len(rights)
    shape = jax.ShapeDtypeStruct((n_right, height, wide), jnp.float32)
    spec = pl.BlockSpec((halves, None, wide, depth), lambda i: (0, piece, 0, 0))
    return pl.pallas_call(
        functools.partial(outer_kernel, len(inners), n_right),
        grid=(1,),
        in_specs=[SCALARS] + [WHOLE] * len(inners) + [spec] * n_right,
        out_specs=[WHOLE, WHOLE],
        out_shape=[shape, shape],
        compiler_params=params(),
        cost_estimate=COST,
    )(side.astype(jnp.int32).reshape(1), *inners, *rights)


def cores_kernel(index_ref, keep_ref, got_ref, kept_ref, sent_ref):
    height = kept_ref.shape[1]
    for k in range(index_ref.shape[0]):
        rows = pl.ds(pl.multiple_of(index_ref[k] * height, height), height)
        for j in range(kept_ref.shape[0]):
            total = keep_ref[j, rows, :] + got_ref[j, rows, :]
            if k == 0:
                kept_ref[j] = total
            else:
                sent_ref[k - 1, j] = total.astype(sent_ref.dtype)


def cores_summed(keep, got, index, height):
    blocks, _, wide = keep.shape
    others = index.shape[0] - 1
    return pl.pallas_call(
        cores_kernel,
        in_specs=[SCALARS, WHOLE, WHOLE],
        out_specs=[WHOLE, WHOLE],
        out_shape=[
            jax.ShapeDtypeStruct((blocks, height, wide), jnp.float32),
            jax.ShapeDtypeStruct((others, blocks, height, wide), jnp.bfloat16),
        ],
        compiler_params=params(),
        cost_estimate=COST,
    )(index, keep, got)


def planes_kernel(n_got, index_ref, kept_ref, *refs):
    got_refs = refs[:n_got]
    final_ref, sent_ref = refs[n_got:]
    for k in range(index_ref.shape[0]):
        block = index_ref[k]
        total = kept_ref[block]
        for ref in got_refs:
            total = total + ref[block].astype(jnp.float32)
        if k == 0:
            final_ref[...] = total
        else:
            sent_ref[k - 1] = total.astype(sent_ref.dtype)


def planes_summed(kept, got, index):
    blocks, height, wide = kept.shape
    return pl.pallas_call(
        functools.partial(planes_kernel, len(got)),
        in_specs=[SCALARS] + [WHOLE] * (1 + len(got)),
        out_specs=[WHOLE, WHOLE],
        out_shape=[
            jax.ShapeDtypeStruct((height, wide), jnp.float32),
            jax.ShapeDtypeStruct((blocks - 1, height, wide), jnp.bfloat16),
        ],
        compiler_params=params(),
        cost_estimate=COST,
    )(index, kept, *got)


def after(value, *earlier):
    return lax.optimization_barrier((value, *earlier))[0]


def shards(psi, left_ops, right_ops, block_mask):
    terms, n = lax.axis_size("term"), lax.axis_size("row")
    s = math.isqrt(n)
    assert s * s == n and terms == 2 * n and left_ops.shape[0] == 1
    height, width = psi.shape
    term, row = lax.axis_index("term"), lax.axis_index("row")
    core, z = term % 2, term // 2
    zh, zl = z // s, z % s
    hi, lo = row // s, row % s

    def from_lo(value, j):
        pairs = [(a * s + (b + j) % s, a * s + b) for a in range(s) for b in range(s)]
        return lax.ppermute(value, "row", pairs)

    def from_hi(value, j):
        pairs = [(((a + j) % s) * s + b, a * s + b) for a in range(s) for b in range(s)]
        return lax.ppermute(value, "row", pairs)

    def from_term(value, bit):
        return lax.ppermute(value, "term", [(a ^ bit, a) for a in range(terms)])

    def to_zl(value, j):
        pairs = [
            ((a * s + b) * 2 + c, (a * s + (b + j) % s) * 2 + c)
            for a in range(s) for b in range(s) for c in range(2)
        ]
        return lax.ppermute(value, "term", pairs)

    def to_zh(value, j):
        pairs = [
            ((a * s + b) * 2 + c, (((a + j) % s) * s + b) * 2 + c)
            for a in range(s) for b in range(s) for c in range(2)
        ]
        return lax.ppermute(value, "term", pairs)

    def crossed(value):
        pairs = [
            (((a * s + b) * 2 + c) * n + y * s + x, ((a * s + x) * 2 + c) * n + y * s + b)
            for a in range(s) for b in range(s) for c in range(2) for y in range(s) for x in range(s)
        ]
        return lax.ppermute(value, ("term", "row"), pairs)

    sharing = min(SHARE, max(1, height // 128))
    share = height // sharing
    mine = term % sharing
    own_share = lax.dynamic_slice_in_dim(psi, mine * share, share, 0)
    depth = n * height

    def place(jy, jx, bits):
        return ((hi + jy) % s * s + (lo + jx) % s) * height + (mine ^ bits) * share

    near_x = [from_lo(own_share, j) for j in range(1, s)]
    near_y = [from_hi(own_share, j) for j in range(1, s)]
    near_x, near_y, own_left = lax.optimization_barrier(
        (near_x, near_y, masked_rows(left_ops[0], block_mask[0]))
    )
    far = [from_hi(v, jy) for jy in range(1, s) for v in near_x]
    at_near = [(0, j) for j in range(1, s)] + [(j, 0) for j in range(1, s)]
    at_far = [(jy, jx) for jy in range(1, s) for jx in range(1, s)]
    near = jnp.concatenate(near_x + near_y, 0)
    far = jnp.concatenate(far, 0)
    first, last = [(at_near, 0, near), (at_far, 0, far)], []
    if sharing > 1:
        near_core = from_term(near, 1)
        first += [(at_near, 1, near_core), (at_far, 1, from_term(far, 1))]
    early = stacked([psi] + [v for _, _, v in first])
    if sharing > 2:
        near_z, far_z = from_term(near, 2), from_term(far, 2)
        last = [(at_near, 2, near_z), (at_far, 2, far_z)]
        last += [(at_near, 3, from_term(after(near_z, early), 1)), (at_far, 3, from_term(far_z, 1))]
    parts = [early] + [v for _, _, v in last]
    held = [place(*at, bits) for group, bits, _ in first + last for at in group]
    sizes = [height] + [share] * len(held)
    places = jnp.stack([row * height] + held).astype(jnp.int32)

    near_left = [from_lo(own_left, j) for j in range(1, s)]
    own_right = after(right_ops[0], far if sharing == 1 else near_core)
    rights = [own_right] + [from_hi(own_right, j) for j in range(1, s)]
    rights = [a.reshape(2, PIECES, height // (2 * PIECES), width) for a in rights]

    inners = [inner_of(own_left, parts, sizes, places)]
    for rows in near_left:
        inners.append(inner_of(after(rows, inners[-1]), parts, sizes, places))

    def members(own, base):
        return jnp.stack([(own + j - base) % s for j in range(s)]).astype(jnp.int32)

    outs = []
    for p in range(PIECES):
        keep, give = outer_of(inners, p, rights, core)
        kept, sent = cores_summed(keep, from_term(give, 1), members(zl, lo), height)
        got = [to_zl(sent[j - 1], j) for j in range(1, s)]
        final, sent = planes_summed(kept, got, members(zh, hi))
        for j in range(1, s):
            final = final + to_zh(sent[j - 1], j).astype(jnp.float32)
        outs.append(crossed(final.astype(jnp.bfloat16)))
    return jnp.concatenate(outs, 1)


def solution(mesh):
    in_specs = (
        P("row", None),
        P("term", "row", None),
        P("term", "row", None),
        P("term", "row", None),
    )
    out_specs = P("row", "term")
    return jax.shard_map(shards, mesh=mesh, in_specs=in_specs, out_specs=out_specs, check_vma=False)
```

```python
import functools
import math

import jax
import jax.numpy as jnp
from jax import lax
from jax.experimental import pallas as pl
from jax.experimental.pallas import tpu as pltpu
from jax.sharding import PartitionSpec as P

SHARE = 4
PIECES = 2
VMEM_BYTES = 20 * 1024 * 1024
COST = pl.CostEstimate(flops=1, bytes_accessed=1, transcendentals=0)
WHOLE = pl.BlockSpec(memory_space=pltpu.VMEM)
SCALARS = pl.BlockSpec(memory_space=pltpu.SMEM)
ANYWHERE = pl.BlockSpec(memory_space=pl.ANY)


def vmem(shape, kind):
    return pltpu.VMEM(shape, kind)


def held(values):
    return [pltpu.with_memory_space_constraint(v, pltpu.VMEM) for v in values]


def params():
    return pltpu.CompilerParams(vmem_limit_bytes=VMEM_BYTES)


def mask_kernel(blk, mask_ref, left_ref, out_ref):
    for j in range(left_ref.shape[1] // blk):
        keep = mask_ref[pl.program_id(0), j] != 0
        cols = pl.ds(j * blk, blk)
        tile = left_ref[:, cols]
        out_ref[:, cols] = jnp.where(keep, tile, jnp.zeros_like(tile))


def masked_rows(left, mask):
    rows, width = left.shape
    blk = width // mask.shape[1]
    spec = pl.BlockSpec((blk, width), lambda i: (i, 0))
    return pl.pallas_call(
        functools.partial(mask_kernel, blk),
        grid=(rows // blk,),
        in_specs=[SCALARS, spec],
        out_specs=spec,
        out_shape=jax.ShapeDtypeStruct((rows, width), left.dtype),
        compiler_params=params(),
        cost_estimate=COST,
    )(mask, left)


def stack_kernel(*refs):
    part_refs, (whole, sems) = refs[:-2], refs[-2:]
    copies, at = [], 0
    for p, part in enumerate(part_refs):
        size = part.shape[0]
        copies.append(pltpu.make_async_copy(part, whole.at[pl.ds(at, size)], sems.at[p]))
        at += size
    for copy in copies:
        copy.start()
    for copy in copies:
        copy.wait()


def stacked(parts):
    depth, width = sum(a.shape[0] for a in parts), parts[0].shape[1]
    return pl.pallas_call(
        stack_kernel,
        in_specs=[ANYWHERE] * len(parts),
        out_specs=ANYWHERE,
        out_shape=vmem((depth, width), parts[0].dtype),
        scratch_shapes=[pltpu.SemaphoreType.DMA((len(parts),))],
        compiler_params=params(),
        cost_estimate=COST,
    )(*parts)


def inner_kernel(sizes, n_parts, place_ref, rows_ref, *refs):
    part_refs, (out_ref, ordered) = refs[:n_parts], refs[n_parts:]
    at = 0
    for p, size in enumerate(sizes):
        cols = pl.ds(pl.multiple_of(place_ref[p], size), size)
        ordered[:, at : at + size] = rows_ref[:, cols]
        at += size
    step = math.gcd(out_ref.shape[1], 512)
    for j in range(out_ref.shape[1] // step):
        cols = pl.ds(j * step, step)
        psi = jnp.concatenate([ref[:, cols] for ref in part_refs], 0)
        value = jnp.dot(ordered[...], psi, preferred_element_type=jnp.float32)
        out_ref[:, cols] = value.astype(out_ref.dtype)


def inner_of(rows, parts, sizes, places):
    height, depth = rows.shape
    width = parts[0].shape[1]
    return pl.pallas_call(
        functools.partial(inner_kernel, sizes, len(parts)),
        in_specs=[SCALARS] + [WHOLE] * (1 + len(parts)),
        out_specs=WHOLE,
        out_shape=vmem((height, width), parts[0].dtype),
        scratch_shapes=[pltpu.VMEM((height, depth), rows.dtype)],
        compiler_params=params(),
        cost_estimate=COST,
    )(places, *held([rows, *parts]))


def outer_kernel(n_inner, pieces, half_ref, *refs):
    inner_refs, right_refs, out_refs = refs[:n_inner], refs[n_inner:-pieces], refs[-pieces:]
    blocks, _, wide = out_refs[0].shape
    right = jnp.concatenate([ref[p] for p in range(pieces) for ref in right_refs], 0)
    at = 0
    for ref in inner_refs:
        value = lax.dot_general(
            ref[...], right, (((1,), (1,)), ((), ())), preferred_element_type=jnp.float32
        )
        for p, out_ref in enumerate(out_refs):
            for j in range(blocks):
                col = (p * blocks + j) * wide
                out_ref[j, at : at + ref.shape[0], :] = value[:, col : col + wide].astype(out_ref.dtype)
        at += ref.shape[0]


def outer_of(inners, rights, half, kind, cost):
    height = sum(a.shape[0] for a in inners)
    _, pieces, wide, depth = rights[0].shape
    spec = pl.BlockSpec((None, pieces, wide, depth), lambda i, half: (half[0], 0, 0, 0))
    return pl.pallas_call(
        functools.partial(outer_kernel, len(inners), pieces),
        grid_spec=pltpu.PrefetchScalarGridSpec(
            num_scalar_prefetch=1,
            grid=(1,),
            in_specs=[WHOLE] * len(inners) + [spec] * len(rights),
            out_specs=[WHOLE] * pieces,
        ),
        out_shape=[vmem((len(rights), height, wide), kind)] * pieces,
        compiler_params=params(),
        cost_estimate=cost,
    )(half.astype(jnp.int32).reshape(1), *held(inners), *rights)


def cores_kernel(index_ref, keep_ref, got_ref, kept_ref, sent_ref):
    height = kept_ref.shape[1]
    for k in range(index_ref.shape[0]):
        rows = pl.ds(pl.multiple_of(index_ref[k] * height, height), height)
        for j in range(kept_ref.shape[0]):
            total = keep_ref[j, rows, :] + got_ref[j, rows, :]
            if k == 0:
                kept_ref[j] = total
            else:
                sent_ref[k - 1, j] = total.astype(sent_ref.dtype)


def cores_summed(keep, got, index, height):
    blocks, _, wide = keep.shape
    others = index.shape[0] - 1
    return pl.pallas_call(
        cores_kernel,
        in_specs=[SCALARS, WHOLE, WHOLE],
        out_specs=[WHOLE, WHOLE],
        out_shape=[
            vmem((blocks, height, wide), jnp.float32),
            vmem((others, blocks, height, wide), jnp.bfloat16),
        ],
        compiler_params=params(),
        cost_estimate=COST,
    )(index, *held([keep, got]))


def chosen_kernel(index_ref, *refs):
    n = index_ref.shape[0]
    for k, out_ref in enumerate(refs[n:]):
        for j in range(out_ref.shape[0]):
            value = refs[0][j].astype(jnp.float32)
            for i in range(1, n):
                value = jnp.where(index_ref[k] == i, refs[i][j].astype(jnp.float32), value)
            out_ref[j] = value.astype(out_ref.dtype)


def chosen_of(values, index):
    kinds = [jnp.float32] + [jnp.bfloat16] * (len(values) - 1)
    return pl.pallas_call(
        chosen_kernel,
        in_specs=[SCALARS] + [WHOLE] * len(values),
        out_specs=[WHOLE] * len(values),
        out_shape=[vmem(values[0].shape, kind) for kind in kinds],
        compiler_params=params(),
        cost_estimate=COST,
    )(index, *held(values))


def planes_kernel(n_got, index_ref, kept_ref, *refs):
    got_refs = refs[:n_got]
    final_ref, sent_ref = refs[n_got:]
    for k in range(index_ref.shape[0]):
        block = index_ref[k]
        total = kept_ref[block]
        for ref in got_refs:
            total = total + ref[block].astype(jnp.float32)
        if k == 0:
            final_ref[...] = total
        else:
            sent_ref[k - 1] = total.astype(sent_ref.dtype)


def planes_summed(kept, got, index):
    blocks, height, wide = kept.shape
    return pl.pallas_call(
        functools.partial(planes_kernel, len(got)),
        in_specs=[SCALARS] + [WHOLE] * (1 + len(got)),
        out_specs=[WHOLE, WHOLE],
        out_shape=[
            vmem((height, wide), jnp.float32),
            vmem((blocks - 1, height, wide), jnp.bfloat16),
        ],
        compiler_params=params(),
        cost_estimate=COST,
    )(index, *held([kept, *got]))


def after(value, *earlier):
    return lax.optimization_barrier((value, *earlier))[0]


def shards(psi, left_ops, right_ops, block_mask):
    terms, n = lax.axis_size("term"), lax.axis_size("row")
    s = math.isqrt(n)
    assert s * s == n and terms == 2 * n and left_ops.shape[0] == 1
    height, width = psi.shape
    term, row = lax.axis_index("term"), lax.axis_index("row")
    core, z = term % 2, term // 2
    zh, zl = z // s, z % s
    hi, lo = row // s, row % s

    def from_lo(value, j):
        pairs = [(a * s + (b + j) % s, a * s + b) for a in range(s) for b in range(s)]
        return lax.ppermute(value, "row", pairs)

    def from_hi(value, j):
        pairs = [(((a + j) % s) * s + b, a * s + b) for a in range(s) for b in range(s)]
        return lax.ppermute(value, "row", pairs)

    def from_term(value, bit):
        return lax.ppermute(value, "term", [(a ^ bit, a) for a in range(terms)])

    def to_zl(value, j):
        pairs = [
            ((a * s + b) * 2 + c, (a * s + (b + j) % s) * 2 + c)
            for a in range(s) for b in range(s) for c in range(2)
        ]
        return lax.ppermute(value, "term", pairs)

    def to_zh(value, j):
        pairs = [
            ((a * s + b) * 2 + c, (((a + j) % s) * s + b) * 2 + c)
            for a in range(s) for b in range(s) for c in range(2)
        ]
        return lax.ppermute(value, "term", pairs)

    def crossed(value):
        pairs = [
            (((a * s + b) * 2 + c) * n + y * s + x, ((a * s + x) * 2 + c) * n + y * s + b)
            for a in range(s) for b in range(s) for c in range(2) for y in range(s) for x in range(s)
        ]
        return lax.ppermute(value, ("term", "row"), pairs)

    sharing = min(SHARE, max(1, height // 128))
    share = height // sharing
    mine = term % sharing
    own_share = lax.dynamic_slice_in_dim(psi, mine * share, share, 0)
    depth = n * height

    def place(jy, jx, bits):
        return ((hi + jy) % s * s + (lo + jx) % s) * height + (mine ^ bits) * share

    near_x = [from_lo(own_share, j) for j in range(1, s)]
    near_y = [from_hi(own_share, j) for j in range(1, s)]
    near_x, near_y, own_left = lax.optimization_barrier(
        (near_x, near_y, masked_rows(left_ops[0], block_mask[0]))
    )
    far = [from_hi(v, jy) for jy in range(1, s) for v in near_x]
    at_near = [(0, j) for j in range(1, s)] + [(j, 0) for j in range(1, s)]
    at_far = [(jy, jx) for jy in range(1, s) for jx in range(1, s)]
    near = jnp.concatenate(near_x + near_y, 0)
    far = jnp.concatenate(far, 0)
    first, last = [(at_near, 0, near), (at_far, 0, far)], []
    if sharing > 1:
        near_core = from_term(near, 1)
        first += [(at_near, 1, near_core), (at_far, 1, from_term(far, 1))]
    early = stacked([psi] + [v for _, _, v in first])
    if sharing > 2:
        near_z, far_z = from_term(near, 2), from_term(far, 2)
        last = [(at_near, 2, near_z), (at_far, 2, far_z)]
        last += [(at_near, 3, from_term(after(near_z, early), 1)), (at_far, 3, from_term(far_z, 1))]
    parts = [early] + [v for _, _, v in last]
    held = [place(*at, bits) for group, bits, _ in first + last for at in group]
    sizes = [height] + [share] * len(held)
    places = jnp.stack([row * height] + held).astype(jnp.int32)

    near_left = [from_lo(own_left, j) for j in range(1, s)]
    own_right = after(right_ops[0], far if sharing == 1 else near_core)
    rights = [own_right] + [from_hi(own_right, j) for j in range(1, s)]
    rights = [a.reshape(2, PIECES, height // (2 * PIECES), width) for a in rights]

    inners = [inner_of(own_left, parts, sizes, places)]
    for rows in near_left:
        inners.append(inner_of(after(rows, inners[-1]), parts, sizes, places))

    def members(own, base):
        return jnp.stack([(own + j - base) % s for j in range(s)]).astype(jnp.int32)

    give = outer_of(inners, rights, 1 - core, jnp.bfloat16, COST)
    got = [from_term(v, 1) for v in give]
    flops = 2 * len(inners) * height * len(rights) * (height // 2) * width
    cost = pl.CostEstimate(flops=flops, bytes_accessed=1, transcendentals=0)
    keep = outer_of(inners, rights, after(core, give), jnp.float32, cost)
    outs = []
    for p in range(PIECES):
        home_first = p % 2 == 0
        index = jnp.arange(s, dtype=jnp.int32) if home_first else members(zl, lo)
        kept, sent = cores_summed(keep[p], got[p], index, height)
        if home_first:
            held_blocks = [kept] + [from_lo(sent[s - j - 1], j) for j in range(1, s)]
            kept, *sent = chosen_of(held_blocks, members(zl, lo))
        final, sent = planes_summed(kept, [to_zl(sent[j - 1], j) for j in range(1, s)], members(zh, hi))
        for j in range(1, s):
            final = final + to_zh(sent[j - 1], j).astype(jnp.float32)
        final = final.astype(jnp.bfloat16)
        outs.append(final if home_first else crossed(final))
    return jnp.concatenate(outs, 1)


def solution(mesh):
    in_specs = (
        P("row", None),
        P("term", "row", None),
        P("term", "row", None),
        P("term", "row", None),
    )
    out_specs = P("row", "term")
    return jax.shard_map(shards, mesh=mesh, in_specs=in_specs, out_specs=out_specs, check_vma=False)
```

```python
import functools
import math

import jax
import jax.numpy as jnp
from jax import lax
from jax.experimental import pallas as pl
from jax.experimental.pallas import tpu as pltpu
from jax.sharding import PartitionSpec as P

SHARE = 4
PIECES = 2
FIRST = (1, 2)
VMEM_BYTES = 20 * 1024 * 1024
COST = pl.CostEstimate(flops=1, bytes_accessed=1, transcendentals=0)
WHOLE = pl.BlockSpec(memory_space=pltpu.VMEM)
SCALARS = pl.BlockSpec(memory_space=pltpu.SMEM)
ANYWHERE = pl.BlockSpec(memory_space=pl.ANY)


def vmem(shape, kind):
    return pltpu.VMEM(shape, kind)


def held(values):
    return [pltpu.with_memory_space_constraint(v, pltpu.VMEM) for v in values]


def params():
    return pltpu.CompilerParams(vmem_limit_bytes=VMEM_BYTES)


def mask_kernel(blk, mask_ref, left_ref, out_ref):
    for j in range(left_ref.shape[1] // blk):
        keep = mask_ref[pl.program_id(0), j] != 0
        cols = pl.ds(j * blk, blk)
        tile = left_ref[:, cols]
        out_ref[:, cols] = jnp.where(keep, tile, jnp.zeros_like(tile))


def masked_rows(left, mask):
    rows, width = left.shape
    blk = width // mask.shape[1]
    spec = pl.BlockSpec((blk, width), lambda i: (i, 0))
    return pl.pallas_call(
        functools.partial(mask_kernel, blk),
        grid=(rows // blk,),
        in_specs=[SCALARS, spec],
        out_specs=spec,
        out_shape=jax.ShapeDtypeStruct((rows, width), left.dtype),
        compiler_params=params(),
        cost_estimate=COST,
    )(mask, left)


def stack_kernel(*refs):
    part_refs, (whole, sems) = refs[:-2], refs[-2:]
    copies, at = [], 0
    for p, part in enumerate(part_refs):
        size = part.shape[0]
        copies.append(pltpu.make_async_copy(part, whole.at[pl.ds(at, size)], sems.at[p]))
        at += size
    for copy in copies:
        copy.start()
    for copy in copies:
        copy.wait()


def stacked(parts):
    depth, width = sum(a.shape[0] for a in parts), parts[0].shape[1]
    return pl.pallas_call(
        stack_kernel,
        in_specs=[ANYWHERE] * len(parts),
        out_specs=ANYWHERE,
        out_shape=vmem((depth, width), parts[0].dtype),
        scratch_shapes=[pltpu.SemaphoreType.DMA((len(parts),))],
        compiler_params=params(),
        cost_estimate=COST,
    )(*parts)


def inner_kernel(sizes, n_parts, place_ref, rows_ref, *refs):
    part_refs, refs = refs[:n_parts], refs[n_parts:]
    copies = []
    if len(refs) > 2:
        half_ref, right_ref, out_ref, right_out, ordered, sems = refs
        for k in range(2):
            half = half_ref[0] if k == 0 else 1 - half_ref[0]
            copies.append(pltpu.make_async_copy(right_ref.at[half], right_out.at[k], sems.at[k]))
            copies[-1].start()
    else:
        out_ref, ordered = refs
    at = 0
    for p, size in enumerate(sizes):
        cols = pl.ds(pl.multiple_of(place_ref[p], size), size)
        ordered[:, at : at + size] = rows_ref[:, cols]
        at += size
    step = math.gcd(out_ref.shape[1], 512)
    for j in range(out_ref.shape[1] // step):
        cols = pl.ds(j * step, step)
        psi = jnp.concatenate([ref[:, cols] for ref in part_refs], 0)
        value = jnp.dot(ordered[...], psi, preferred_element_type=jnp.float32)
        out_ref[:, cols] = value.astype(out_ref.dtype)
    for copy in copies:
        copy.wait()


def inner_of(rows, parts, sizes, places, right=None, half=None):
    height, depth = rows.shape
    kind = parts[0].dtype
    shape, extra, scratch = [vmem((height, parts[0].shape[1]), kind)], [], [pltpu.VMEM((height, depth), kind)]
    if right is not None:
        shape.append(vmem(right.shape, kind))
        extra = [half.astype(jnp.int32).reshape(1), right]
        scratch.append(pltpu.SemaphoreType.DMA((2,)))
    return pl.pallas_call(
        functools.partial(inner_kernel, sizes, len(parts)),
        in_specs=[SCALARS] + [WHOLE] * (1 + len(parts)) + [SCALARS, ANYWHERE][: len(extra)],
        out_specs=[WHOLE] * len(shape),
        out_shape=shape,
        scratch_shapes=scratch,
        compiler_params=params(),
        cost_estimate=COST,
    )(places, *held([rows, *parts]), *extra)


def products(inner_refs, right, outs, j):
    for e, ref in enumerate(inner_refs):
        value = lax.dot_general(
            ref[...], right, (((1,), (1,)), ((), ())), preferred_element_type=jnp.float32
        )
        at = 0
        for out_ref in outs:
            size = out_ref.shape[2]
            out_ref[j, e] = value[at : at + size, :].astype(out_ref.dtype)
            at += size


def give_kernel(n_inner, n_near, half_ref, *refs):
    inner_refs, own_ref, near_refs = refs[:n_inner], refs[n_inner], refs[n_inner + 1 : n_inner + 1 + n_near]
    outs, kept_refs = refs[n_inner + 1 + n_near :][:PIECES], refs[n_inner + 1 + n_near + PIECES : -2]
    held_ref, sems = refs[-2:]
    copies = []
    for k, targets in enumerate(([held_ref.at[j] for j in range(n_near)], kept_refs)):
        half = half_ref[0] if k == 0 else 1 - half_ref[0]
        for j, (ref, target) in enumerate(zip(near_refs, targets)):
            copies.append(pltpu.make_async_copy(ref.at[half], target, sems.at[k, j]))
            copies[-1].start()
    products(inner_refs, own_ref[0], outs, 0)
    for j in range(n_near):
        copies[j].wait()
        products(inner_refs, held_ref[j], outs, 1 + j)
    for copy in copies[n_near:]:
        copy.wait()


def give_of(inners, own, nears, half, sizes):
    _, rows, depth = own.shape
    made = pl.pallas_call(
        functools.partial(give_kernel, len(inners), len(nears)),
        in_specs=[SCALARS] + [WHOLE] * (len(inners) + 1) + [ANYWHERE] * len(nears),
        out_specs=[WHOLE] * (PIECES + len(nears)),
        out_shape=[vmem((1 + len(nears), len(inners), size, rows), jnp.bfloat16) for size in sizes]
        + [vmem((rows, depth), own.dtype)] * len(nears),
        scratch_shapes=[
            pltpu.VMEM((len(nears), rows, depth), own.dtype),
            pltpu.SemaphoreType.DMA((2, len(nears))),
        ],
        compiler_params=params(),
        cost_estimate=COST,
    )(half.astype(jnp.int32).reshape(1), *held([*inners, own]), *nears)
    return made[:PIECES], made[PIECES:]


def keep_kernel(n_inner, *refs):
    inner_refs, own_ref, rest = refs[:n_inner], refs[n_inner], refs[n_inner + 1 :]
    near_refs, outs = rest[:-PIECES], rest[-PIECES:]
    products(inner_refs, own_ref[1], outs, 0)
    for j, ref in enumerate(near_refs):
        products(inner_refs, ref[...], outs, 1 + j)


def keep_of(inners, own, nears, sizes):
    height = sum(a.shape[0] for a in inners)
    _, rows, depth = own.shape
    flops = 2 * height * (1 + len(nears)) * rows * depth
    return pl.pallas_call(
        functools.partial(keep_kernel, len(inners)),
        in_specs=[WHOLE] * (len(inners) + 1 + len(nears)),
        out_specs=[WHOLE] * PIECES,
        out_shape=[vmem((1 + len(nears), len(inners), size, rows), jnp.float32) for size in sizes],
        compiler_params=params(),
        cost_estimate=pl.CostEstimate(flops=flops, bytes_accessed=1, transcendentals=0),
    )(*held([*inners, own, *nears]))


def cores_kernel(index_ref, keep_ref, got_ref, kept_ref, sent_ref):
    for k in range(index_ref.shape[0]):
        block = index_ref[k]
        for j in range(kept_ref.shape[0]):
            total = keep_ref[j, block] + got_ref[j, block]
            if k == 0:
                kept_ref[j] = total
            else:
                sent_ref[k - 1, j] = total.astype(sent_ref.dtype)


def cores_summed(keep, got, index):
    blocks, _, height, wide = keep.shape
    others = index.shape[0] - 1
    return pl.pallas_call(
        cores_kernel,
        in_specs=[SCALARS, WHOLE, WHOLE],
        out_specs=[WHOLE, WHOLE],
        out_shape=[
            vmem((blocks, height, wide), jnp.float32),
            vmem((others, blocks, height, wide), jnp.bfloat16),
        ],
        compiler_params=params(),
        cost_estimate=COST,
    )(index, *held([keep, got]))


def chosen_kernel(index_ref, *refs):
    n = index_ref.shape[0]
    for k, out_ref in enumerate(refs[n:]):
        for j in range(out_ref.shape[0]):
            value = refs[0][j].astype(jnp.float32)
            for i in range(1, n):
                value = jnp.where(index_ref[k] == i, refs[i][j].astype(jnp.float32), value)
            out_ref[j] = value.astype(out_ref.dtype)


def chosen_of(values, index):
    kinds = [jnp.float32] + [jnp.bfloat16] * (len(values) - 1)
    return pl.pallas_call(
        chosen_kernel,
        in_specs=[SCALARS] + [WHOLE] * len(values),
        out_specs=[WHOLE] * len(values),
        out_shape=[vmem(values[0].shape, kind) for kind in kinds],
        compiler_params=params(),
        cost_estimate=COST,
    )(index, *held(values))


def planes_kernel(n_got, index_ref, kept_ref, *refs):
    got_refs = refs[:n_got]
    final_ref, sent_ref = refs[n_got:]
    for k in range(index_ref.shape[0]):
        block = index_ref[k]
        total = kept_ref[block]
        for ref in got_refs:
            total = total + ref[block].astype(jnp.float32)
        if k == 0:
            final_ref[...] = total
        else:
            sent_ref[k - 1] = total.astype(sent_ref.dtype)


def planes_summed(kept, got, index):
    blocks, height, wide = kept.shape
    return pl.pallas_call(
        functools.partial(planes_kernel, len(got)),
        in_specs=[SCALARS] + [WHOLE] * (1 + len(got)),
        out_specs=[WHOLE, WHOLE],
        out_shape=[
            vmem((height, wide), jnp.float32),
            vmem((blocks - 1, height, wide), jnp.bfloat16),
        ],
        compiler_params=params(),
        cost_estimate=COST,
    )(index, *held([kept, *got]))


def after(value, *earlier):
    return lax.optimization_barrier((value, *earlier))[0]


def shards(psi, left_ops, right_ops, block_mask):
    terms, n = lax.axis_size("term"), lax.axis_size("row")
    s = math.isqrt(n)
    assert s * s == n and terms == 2 * n and left_ops.shape[0] == 1
    height, width = psi.shape
    term, row = lax.axis_index("term"), lax.axis_index("row")
    core, z = term % 2, term // 2
    zh, zl = z // s, z % s
    hi, lo = row // s, row % s

    def from_lo(value, j):
        pairs = [(a * s + (b + j) % s, a * s + b) for a in range(s) for b in range(s)]
        return lax.ppermute(value, "row", pairs)

    def from_hi(value, j):
        pairs = [(((a + j) % s) * s + b, a * s + b) for a in range(s) for b in range(s)]
        return lax.ppermute(value, "row", pairs)

    def from_term(value, bit):
        return lax.ppermute(value, "term", [(a ^ bit, a) for a in range(terms)])

    def to_zl(value, j):
        pairs = [
            ((a * s + b) * 2 + c, (a * s + (b + j) % s) * 2 + c)
            for a in range(s) for b in range(s) for c in range(2)
        ]
        return lax.ppermute(value, "term", pairs)

    def to_zh(value, j):
        pairs = [
            ((a * s + b) * 2 + c, (((a + j) % s) * s + b) * 2 + c)
            for a in range(s) for b in range(s) for c in range(2)
        ]
        return lax.ppermute(value, "term", pairs)

    def crossed(value):
        pairs = [
            (((a * s + b) * 2 + c) * n + y * s + x, ((a * s + x) * 2 + c) * n + y * s + b)
            for a in range(s) for b in range(s) for c in range(2) for y in range(s) for x in range(s)
        ]
        return lax.ppermute(value, ("term", "row"), pairs)

    sharing = min(SHARE, max(1, height // 128))
    share = height // sharing
    mine = term % sharing
    own_share = lax.dynamic_slice_in_dim(psi, mine * share, share, 0)
    depth = n * height

    def place(jy, jx, bits):
        return ((hi + jy) % s * s + (lo + jx) % s) * height + (mine ^ bits) * share

    near_x = [from_lo(own_share, j) for j in range(1, s)]
    near_y = [from_hi(own_share, j) for j in range(1, s)]
    near_x, near_y, own_left = lax.optimization_barrier(
        (near_x, near_y, masked_rows(left_ops[0], block_mask[0]))
    )
    far = [from_hi(v, jy) for jy in range(1, s) for v in near_x]
    at_near = [(0, j) for j in range(1, s)] + [(j, 0) for j in range(1, s)]
    at_far = [(jy, jx) for jy in range(1, s) for jx in range(1, s)]
    near = jnp.concatenate(near_x + near_y, 0)
    far = jnp.concatenate(far, 0)
    first, last = [(at_near, 0, near), (at_far, 0, far)], []
    if sharing > 1:
        near_core = from_term(near, 1)
        first += [(at_near, 1, near_core), (at_far, 1, from_term(far, 1))]
    early = stacked([psi] + [v for _, _, v in first])
    if sharing > 2:
        near_z, far_z = from_term(near, 2), from_term(far, 2)
        last = [(at_near, 2, near_z), (at_far, 2, far_z)]
        last += [(at_near, 3, from_term(after(near_z, early), 1)), (at_far, 3, from_term(far_z, 1))]
    parts = [early] + [v for _, _, v in last]
    held = [place(*at, bits) for group, bits, _ in first + last for at in group]
    sizes = [height] + [share] * len(held)
    places = jnp.stack([row * height] + held).astype(jnp.int32)

    near_left = [from_lo(own_left, j) for j in range(1, s)]
    own_right = after(right_ops[0], far if sharing == 1 else near_core)
    rights = [own_right] + [from_hi(own_right, j) for j in range(1, s)]
    rights = [a.reshape(2, height // 2, width) for a in rights]

    inners = list(inner_of(own_left, parts, sizes, places))
    for rows in near_left:
        rows = after(rows, inners[-1])
        inner, own_halves = inner_of(rows, parts, sizes, places, rights[0], 1 - core)
        inners.append(inner)

    def members(own, base):
        return jnp.stack([(own + j - base) % s for j in range(s)]).astype(jnp.int32)

    cut = height * FIRST[0] // FIRST[1] // 32 * 32
    row_sizes = [cut, height - cut]
    give, near_halves = give_of(inners, own_halves, rights[1:], 1 - core, row_sizes)
    got = [from_term(v, 1) for v in give]
    keep = keep_of(inners, own_halves, near_halves, row_sizes)
    outs = []
    for p in range(PIECES):
        home_first = p % 2 == 0
        index = jnp.arange(s, dtype=jnp.int32) if home_first else members(zl, lo)
        kept, sent = cores_summed(keep[p], got[p], index)
        if home_first:
            held_blocks = [kept] + [from_lo(sent[s - j - 1], j) for j in range(1, s)]
            kept, *sent = chosen_of(held_blocks, members(zl, lo))
        final, sent = planes_summed(kept, [to_zl(sent[j - 1], j) for j in range(1, s)], members(zh, hi))
        for j in range(1, s):
            final = final + to_zh(sent[j - 1], j).astype(jnp.float32)
        final = final.astype(jnp.bfloat16)
        outs.append(final if home_first else crossed(final))
    return jnp.concatenate(outs, 0)


def solution(mesh):
    in_specs = (
        P("row", None),
        P("term", "row", None),
        P("term", "row", None),
        P("term", "row", None),
    )
    out_specs = P("row", "term")
    return jax.shard_map(shards, mesh=mesh, in_specs=in_specs, out_specs=out_specs, check_vma=False)
```

```python
import functools
import math

import jax
import jax.numpy as jnp
from jax import lax
from jax.experimental import pallas as pl
from jax.experimental.pallas import tpu as pltpu
from jax.sharding import PartitionSpec as P

SHARE = 4
PIECES = 2
FIRST = (9, 16)
VMEM_BYTES = 20 * 1024 * 1024
COST = pl.CostEstimate(flops=1, bytes_accessed=1, transcendentals=0)
WHOLE = pl.BlockSpec(memory_space=pltpu.VMEM)
SCALARS = pl.BlockSpec(memory_space=pltpu.SMEM)
ANYWHERE = pl.BlockSpec(memory_space=pl.ANY)


def vmem(shape, kind):
    return pltpu.VMEM(shape, kind)


def held(values):
    return [pltpu.with_memory_space_constraint(v, pltpu.VMEM) for v in values]


def params():
    return pltpu.CompilerParams(vmem_limit_bytes=VMEM_BYTES)


def mask_kernel(blk, mask_ref, left_ref, out_ref):
    for j in range(left_ref.shape[1] // blk):
        keep = mask_ref[pl.program_id(0), j] != 0
        cols = pl.ds(j * blk, blk)
        tile = left_ref[:, cols]
        out_ref[:, cols] = jnp.where(keep, tile, jnp.zeros_like(tile))


def masked_rows(left, mask):
    rows, width = left.shape
    blk = width // mask.shape[1]
    spec = pl.BlockSpec((blk, width), lambda i: (i, 0))
    return pl.pallas_call(
        functools.partial(mask_kernel, blk),
        grid=(rows // blk,),
        in_specs=[SCALARS, spec],
        out_specs=spec,
        out_shape=jax.ShapeDtypeStruct((rows, width), left.dtype),
        compiler_params=params(),
        cost_estimate=COST,
    )(mask, left)


def share_kernel(start_ref, whole_ref, out_ref, sem):
    size = out_ref.shape[0]
    where = pl.ds(pl.multiple_of(start_ref[0], size), size)
    copy = pltpu.make_async_copy(whole_ref.at[where], out_ref, sem)
    copy.start()
    copy.wait()


def share_of(whole, start, size):
    return pl.pallas_call(
        share_kernel,
        in_specs=[SCALARS, ANYWHERE],
        out_specs=WHOLE,
        out_shape=vmem((size, whole.shape[1]), whole.dtype),
        scratch_shapes=[pltpu.SemaphoreType.DMA],
        compiler_params=params(),
        cost_estimate=COST,
    )(start.astype(jnp.int32).reshape(1), pltpu.with_memory_space_constraint(whole, pltpu.HBM))


def stack_kernel(*refs):
    part_refs, (whole, sems) = refs[:-2], refs[-2:]
    copies, at = [], 0
    for p, part in enumerate(part_refs):
        size = part.shape[0]
        copies.append(pltpu.make_async_copy(part, whole.at[pl.ds(at, size)], sems.at[p]))
        at += size
    for copy in copies:
        copy.start()
    for copy in copies:
        copy.wait()


def stacked(parts):
    depth, width = sum(a.shape[0] for a in parts), parts[0].shape[1]
    return pl.pallas_call(
        stack_kernel,
        in_specs=[ANYWHERE] * len(parts),
        out_specs=ANYWHERE,
        out_shape=vmem((depth, width), parts[0].dtype),
        scratch_shapes=[pltpu.SemaphoreType.DMA((len(parts),))],
        compiler_params=params(),
        cost_estimate=COST,
    )(*parts)


def inner_kernel(sizes, n_parts, place_ref, rows_ref, *refs):
    part_refs, refs = refs[:n_parts], refs[n_parts:]
    copies = []
    if len(refs) > 2:
        half_ref, right_ref, out_ref, right_out, ordered, sems = refs
        for k in range(2):
            half = half_ref[0] if k == 0 else 1 - half_ref[0]
            copies.append(pltpu.make_async_copy(right_ref.at[half], right_out.at[k], sems.at[k]))
            copies[-1].start()
    else:
        out_ref, ordered = refs
    at = 0
    for p, size in enumerate(sizes):
        cols = pl.ds(pl.multiple_of(place_ref[p], size), size)
        ordered[:, at : at + size] = rows_ref[:, cols]
        at += size
    step = math.gcd(out_ref.shape[1], 512)
    for j in range(out_ref.shape[1] // step):
        cols = pl.ds(j * step, step)
        psi = jnp.concatenate([ref[:, cols] for ref in part_refs], 0)
        value = jnp.dot(ordered[...], psi, preferred_element_type=jnp.float32)
        out_ref[:, cols] = value.astype(out_ref.dtype)
    for copy in copies:
        copy.wait()


def inner_of(rows, parts, sizes, places, right=None, half=None):
    height, depth = rows.shape
    kind = parts[0].dtype
    shape, extra, scratch = [vmem((height, parts[0].shape[1]), kind)], [], [pltpu.VMEM((height, depth), kind)]
    if right is not None:
        shape.append(vmem(right.shape, kind))
        extra = [half, right]
        scratch.append(pltpu.SemaphoreType.DMA((2,)))
    return pl.pallas_call(
        functools.partial(inner_kernel, sizes, len(parts)),
        in_specs=[SCALARS] + [WHOLE] * (1 + len(parts)) + [SCALARS, ANYWHERE][: len(extra)],
        out_specs=[WHOLE] * len(shape),
        out_shape=shape,
        scratch_shapes=scratch,
        compiler_params=params(),
        cost_estimate=COST,
    )(places, *held([rows, *parts]), *extra)


def products(inner_refs, right, outs, j):
    for e, ref in enumerate(inner_refs):
        value = lax.dot_general(
            ref[...], right, (((1,), (1,)), ((), ())), preferred_element_type=jnp.float32
        )
        at = 0
        for out_ref in outs:
            size = out_ref.shape[2]
            out_ref[j, e] = value[at : at + size, :].astype(out_ref.dtype)
            at += size


def own_kernel(n_inner, *refs):
    inner_refs, own_ref, outs = refs[:n_inner], refs[n_inner], refs[n_inner + 1 :]
    products(inner_refs, own_ref[0], outs[:PIECES], 0)
    products(inner_refs, own_ref[1], outs[PIECES:], 0)


def give_kernel(n_inner, n_near, half_ref, *refs):
    inner_refs, near_refs, refs = refs[:n_inner], refs[n_inner : n_inner + n_near], refs[n_inner + n_near :]
    outs, kept_refs, (held_ref, sems) = refs[:PIECES], refs[PIECES:-2], refs[-2:]
    copies = []
    for k, targets in enumerate(([held_ref.at[j] for j in range(n_near)], kept_refs)):
        half = half_ref[0] if k == 0 else 1 - half_ref[0]
        for j, (ref, target) in enumerate(zip(near_refs, targets)):
            copies.append(pltpu.make_async_copy(ref.at[half], target, sems.at[k, j]))
            copies[-1].start()
    for j in range(n_near):
        copies[j].wait()
        products(inner_refs, held_ref[j], outs, j)
    for copy in copies[n_near:]:
        copy.wait()


def keep_kernel(n_inner, *refs):
    inner_refs, near_refs, outs = refs[:n_inner], refs[n_inner:-PIECES], refs[-PIECES:]
    for j, ref in enumerate(near_refs):
        products(inner_refs, ref[...], outs, j)


def outer_of(inners, own, nears, half, sizes):
    _, rows, depth = own.shape
    n = len(nears)

    def shapes(blocks, kind):
        return [vmem((blocks, len(inners), size, rows), kind) for size in sizes]

    made = pl.pallas_call(
        functools.partial(own_kernel, len(inners)),
        in_specs=[WHOLE] * (len(inners) + 1),
        out_specs=[WHOLE] * (2 * PIECES),
        out_shape=shapes(1, jnp.bfloat16) + shapes(1, jnp.float32),
        compiler_params=params(),
        cost_estimate=COST,
    )(*held([*inners, own]))
    give, keep = [list(made[:PIECES])], [list(made[PIECES:])]
    made = pl.pallas_call(
        functools.partial(give_kernel, len(inners), n),
        in_specs=[SCALARS] + [WHOLE] * len(inners) + [ANYWHERE] * n,
        out_specs=[WHOLE] * (PIECES + n),
        out_shape=shapes(n, jnp.bfloat16) + [vmem((rows, depth), own.dtype)] * n,
        scratch_shapes=[pltpu.VMEM((n, rows, depth), own.dtype), pltpu.SemaphoreType.DMA((2, n))],
        compiler_params=params(),
        cost_estimate=COST,
    )(half, *held(inners), *after(nears, made))
    give.append(list(made[:PIECES]))
    flops = 2 * sum(sizes) * len(inners) * n * rows * depth
    made = pl.pallas_call(
        functools.partial(keep_kernel, len(inners)),
        in_specs=[WHOLE] * (len(inners) + n),
        out_specs=[WHOLE] * PIECES,
        out_shape=shapes(n, jnp.float32),
        compiler_params=params(),
        cost_estimate=pl.CostEstimate(flops=flops, bytes_accessed=1, transcendentals=0),
    )(*held([*inners, *made[PIECES:]]))
    keep.append(list(made))
    return give, keep


def cores_kernel(index_ref, *refs):
    (own_ref, near_ref), (got_own_ref, got_near_ref), (kept_ref, sent_ref) = refs[:2], refs[2:4], refs[4:]
    for k in range(index_ref.shape[0]):
        block = index_ref[k]
        for j in range(kept_ref.shape[0]):
            if j == 0:
                total = own_ref[0, block] + got_own_ref[0, block]
            else:
                total = near_ref[j - 1, block] + got_near_ref[j - 1, block]
            if k == 0:
                kept_ref[j] = total
            else:
                sent_ref[k - 1, j] = total.astype(sent_ref.dtype)


def cores_summed(keep, got, index):
    near, _, height, wide = keep[1].shape
    others = index.shape[0] - 1
    return pl.pallas_call(
        cores_kernel,
        in_specs=[SCALARS] + [WHOLE] * 4,
        out_specs=[WHOLE, WHOLE],
        out_shape=[
            vmem((1 + near, height, wide), jnp.float32),
            vmem((others, 1 + near, height, wide), jnp.bfloat16),
        ],
        compiler_params=params(),
        cost_estimate=COST,
    )(index, *held([*keep, *got]))


def chosen_kernel(index_ref, *refs):
    n = index_ref.shape[0]
    for k, out_ref in enumerate(refs[n:]):
        for j in range(out_ref.shape[0]):
            value = refs[0][j].astype(jnp.float32)
            for i in range(1, n):
                value = jnp.where(index_ref[k] == i, refs[i][j].astype(jnp.float32), value)
            out_ref[j] = value.astype(out_ref.dtype)


def chosen_of(values, index):
    kinds = [jnp.float32] + [jnp.bfloat16] * (len(values) - 1)
    return pl.pallas_call(
        chosen_kernel,
        in_specs=[SCALARS] + [WHOLE] * len(values),
        out_specs=[WHOLE] * len(values),
        out_shape=[vmem(values[0].shape, kind) for kind in kinds],
        compiler_params=params(),
        cost_estimate=COST,
    )(index, *held(values))


def planes_kernel(n_got, index_ref, kept_ref, *refs):
    got_refs = refs[:n_got]
    final_ref, sent_ref = refs[n_got:]
    for k in range(index_ref.shape[0]):
        block = index_ref[k]
        total = kept_ref[block]
        for ref in got_refs:
            total = total + ref[block].astype(jnp.float32)
        if k == 0:
            final_ref[...] = total
        else:
            sent_ref[k - 1] = total.astype(sent_ref.dtype)


def planes_summed(kept, got, index):
    blocks, height, wide = kept.shape
    return pl.pallas_call(
        functools.partial(planes_kernel, len(got)),
        in_specs=[SCALARS] + [WHOLE] * (1 + len(got)),
        out_specs=[WHOLE, WHOLE],
        out_shape=[
            vmem((height, wide), jnp.float32),
            vmem((blocks - 1, height, wide), jnp.bfloat16),
        ],
        compiler_params=params(),
        cost_estimate=COST,
    )(index, *held([kept, *got]))


def after(value, *earlier):
    return lax.optimization_barrier((value, *earlier))[0]


def shards(psi, left_ops, right_ops, block_mask):
    terms, n = lax.axis_size("term"), lax.axis_size("row")
    s = math.isqrt(n)
    assert s * s == n and terms == 2 * n and left_ops.shape[0] == 1
    height, width = psi.shape
    term, row = lax.axis_index("term"), lax.axis_index("row")
    core, z = term % 2, term // 2
    zh, zl = z // s, z % s
    hi, lo = row // s, row % s

    def from_lo(value, j):
        pairs = [(a * s + (b + j) % s, a * s + b) for a in range(s) for b in range(s)]
        return lax.ppermute(value, "row", pairs)

    def from_hi(value, j):
        pairs = [(((a + j) % s) * s + b, a * s + b) for a in range(s) for b in range(s)]
        return lax.ppermute(value, "row", pairs)

    def from_term(value, bit):
        return lax.ppermute(value, "term", [(a ^ bit, a) for a in range(terms)])

    def to_zl(value, j):
        pairs = [
            ((a * s + b) * 2 + c, (a * s + (b + j) % s) * 2 + c)
            for a in range(s) for b in range(s) for c in range(2)
        ]
        return lax.ppermute(value, "term", pairs)

    def to_zh(value, j):
        pairs = [
            ((a * s + b) * 2 + c, (((a + j) % s) * s + b) * 2 + c)
            for a in range(s) for b in range(s) for c in range(2)
        ]
        return lax.ppermute(value, "term", pairs)

    def crossed(value):
        pairs = [
            (((a * s + b) * 2 + c) * n + y * s + x, ((a * s + x) * 2 + c) * n + y * s + b)
            for a in range(s) for b in range(s) for c in range(2) for y in range(s) for x in range(s)
        ]
        return lax.ppermute(value, ("term", "row"), pairs)

    sharing = min(SHARE, max(1, height // 128))
    share = height // sharing
    mine = term % sharing
    own_share = share_of(psi, mine * share, share)
    depth = n * height

    near_x = [from_lo(own_share, j) for j in range(1, s)]
    near_y = [from_hi(own_share, j) for j in range(1, s)]
    own_share, term, row = lax.optimization_barrier((own_share, term, row))
    core, z, mine = term % 2, term // 2, term % sharing
    zh, zl, hi, lo = z // s, z % s, row // s, row % s

    def place(jy, jx, bits):
        return ((hi + jy) % s * s + (lo + jx) % s) * height + (mine ^ bits) * share

    def members(own, base):
        return jnp.stack([(own + j - base) % s for j in range(s)]).astype(jnp.int32)

    at_near = [(0, j) for j in range(1, s)] + [(j, 0) for j in range(1, s)]
    at_far = [(jy, jx) for jy in range(1, s) for jx in range(1, s)]
    held = [place(*at, bits) for bits in range(sharing) for at in at_near + at_far]
    sizes = [height] + [share] * len(held)
    places = jnp.stack([row * height] + held).astype(jnp.int32)
    half = (1 - core).astype(jnp.int32).reshape(1)
    counted = jnp.arange(s, dtype=jnp.int32)
    near_x, near_y, own_left, places, half, by_zl, by_zh, counted = lax.optimization_barrier(
        (near_x, near_y, masked_rows(left_ops[0], block_mask[0]), places, half, members(zl, lo), members(zh, hi), counted)
    )
    far = [from_hi(v, jy) for jy in range(1, s) for v in near_x]
    near = jnp.concatenate(near_x + near_y, 0)
    far = stacked(far) if len(far) > 1 else far[0]
    first, last = [(at_near, 0, near), (at_far, 0, far)], []
    if sharing > 1:
        near_core = from_term(near, 1)
        first += [(at_near, 1, near_core), (at_far, 1, from_term(far, 1))]
    early = stacked([psi] + [v for _, _, v in first])
    if sharing > 2:
        near_z, far_z = from_term(near, 2), from_term(far, 2)
        last = [(at_near, 2, near_z), (at_far, 2, far_z)]
        last += [(at_near, 3, from_term(after(near_z, early), 1)), (at_far, 3, from_term(far_z, 1))]
    parts = [early] + [v for _, _, v in last]

    near_left = [from_lo(own_left, j) for j in range(1, s)]
    own_right = after(right_ops[0], far if sharing == 1 else near_core)
    rights = [own_right] + [from_hi(own_right, j) for j in range(1, s)]
    rights = [a.reshape(2, height // 2, width) for a in rights]

    inners = list(inner_of(own_left, parts, sizes, places))
    for rows in near_left:
        rows = after(rows, inners[-1])
        inner, own_halves = inner_of(rows, parts, sizes, places, rights[0], half)
        inners.append(inner)

    cut = height * FIRST[0] // FIRST[1] // 32 * 32
    row_sizes = [cut, height - cut]
    give, keep = outer_of(inners, own_halves, rights[1:], half, row_sizes)
    got = [[from_term(v, 1) for v in group] for group in give]
    outs = []
    for p in range(PIECES):
        home_first = p % 2 == 1
        index = counted if home_first else by_zl
        kept, sent = cores_summed([v[p] for v in keep], [v[p] for v in got], index)
        if home_first:
            held_blocks = [kept] + [from_lo(sent[s - j - 1], j) for j in range(1, s)]
            kept, *sent = chosen_of(held_blocks, by_zl)
        final, sent = planes_summed(kept, [to_zl(sent[j - 1], j) for j in range(1, s)], by_zh)
        for j in range(1, s):
            final = final + to_zh(sent[j - 1], j).astype(jnp.float32)
        final = final.astype(jnp.bfloat16)
        outs.append(final if home_first else crossed(final))
    return jnp.concatenate(outs, 0)


def solution(mesh):
    in_specs = (
        P("row", None),
        P("term", "row", None),
        P("term", "row", None),
        P("term", "row", None),
    )
    out_specs = P("row", "term")
    return jax.shard_map(shards, mesh=mesh, in_specs=in_specs, out_specs=out_specs, check_vma=False)
```

```python
import functools
import math

import jax
import jax.numpy as jnp
from jax import lax
from jax.experimental import pallas as pl
from jax.experimental.pallas import tpu as pltpu
from jax.sharding import PartitionSpec as P

SHARE = 4
PIECES = 2
FIRST = (9, 16)
VMEM_BYTES = 20 * 1024 * 1024
COST = pl.CostEstimate(flops=1, bytes_accessed=1, transcendentals=0)
WHOLE = pl.BlockSpec(memory_space=pltpu.VMEM)
SCALARS = pl.BlockSpec(memory_space=pltpu.SMEM)
ANYWHERE = pl.BlockSpec(memory_space=pl.ANY)


def vmem(shape, kind):
    return pltpu.VMEM(shape, kind)


def held(values):
    return [pltpu.with_memory_space_constraint(v, pltpu.VMEM) for v in values]


def params():
    return pltpu.CompilerParams(vmem_limit_bytes=VMEM_BYTES)


def mask_kernel(blk, mask_ref, left_ref, out_ref):
    for j in range(left_ref.shape[1] // blk):
        keep = mask_ref[pl.program_id(0), j] != 0
        cols = pl.ds(j * blk, blk)
        tile = left_ref[:, cols]
        out_ref[:, cols] = jnp.where(keep, tile, jnp.zeros_like(tile))


def masked_rows(left, mask):
    rows, width = left.shape
    blk = width // mask.shape[1]
    spec = pl.BlockSpec((blk, width), lambda i: (i, 0))
    return pl.pallas_call(
        functools.partial(mask_kernel, blk),
        grid=(rows // blk,),
        in_specs=[SCALARS, spec],
        out_specs=spec,
        out_shape=jax.ShapeDtypeStruct((rows, width), left.dtype),
        compiler_params=params(),
        cost_estimate=COST,
    )(mask, left)


def share_kernel(start_ref, whole_ref, out_ref, sem):
    size = out_ref.shape[0]
    where = pl.ds(pl.multiple_of(start_ref[0], size), size)
    copy = pltpu.make_async_copy(whole_ref.at[where], out_ref, sem)
    copy.start()
    copy.wait()


def share_of(whole, start, size):
    return pl.pallas_call(
        share_kernel,
        in_specs=[SCALARS, ANYWHERE],
        out_specs=WHOLE,
        out_shape=vmem((size, whole.shape[1]), whole.dtype),
        scratch_shapes=[pltpu.SemaphoreType.DMA],
        compiler_params=params(),
        cost_estimate=COST,
    )(start.astype(jnp.int32).reshape(1), pltpu.with_memory_space_constraint(whole, pltpu.HBM))


def stack_kernel(*refs):
    part_refs, (whole, sems) = refs[:-2], refs[-2:]
    copies, at = [], 0
    for p, part in enumerate(part_refs):
        size = part.shape[0]
        copies.append(pltpu.make_async_copy(part, whole.at[pl.ds(at, size)], sems.at[p]))
        at += size
    for copy in copies:
        copy.start()
    for copy in copies:
        copy.wait()


def stacked(parts):
    depth, width = sum(a.shape[0] for a in parts), parts[0].shape[1]
    return pl.pallas_call(
        stack_kernel,
        in_specs=[ANYWHERE] * len(parts),
        out_specs=ANYWHERE,
        out_shape=vmem((depth, width), parts[0].dtype),
        scratch_shapes=[pltpu.SemaphoreType.DMA((len(parts),))],
        compiler_params=params(),
        cost_estimate=COST,
    )(*parts)


def inner_kernel(sizes, n_parts, place_ref, rows_ref, *refs):
    part_refs, refs = refs[:n_parts], refs[n_parts:]
    copies = []
    if len(refs) > 2:
        half_ref, right_ref, out_ref, right_out, ordered, sems = refs
        for k in range(2):
            half = half_ref[0] if k == 0 else 1 - half_ref[0]
            copies.append(pltpu.make_async_copy(right_ref.at[half], right_out.at[k], sems.at[k]))
            copies[-1].start()
    else:
        out_ref, ordered = refs
    at = 0
    for p, size in enumerate(sizes):
        cols = pl.ds(pl.multiple_of(place_ref[p], size), size)
        ordered[:, at : at + size] = rows_ref[:, cols]
        at += size
    step = math.gcd(out_ref.shape[1], 512)
    for j in range(out_ref.shape[1] // step):
        cols = pl.ds(j * step, step)
        psi = jnp.concatenate([ref[:, cols] for ref in part_refs], 0)
        value = jnp.dot(ordered[...], psi, preferred_element_type=jnp.float32)
        out_ref[:, cols] = value.astype(out_ref.dtype)
    for copy in copies:
        copy.wait()


def inner_of(rows, parts, sizes, places, right=None, half=None):
    height, depth = rows.shape
    kind = parts[0].dtype
    shape, extra, scratch = [vmem((height, parts[0].shape[1]), kind)], [], [pltpu.VMEM((height, depth), kind)]
    if right is not None:
        shape.append(vmem(right.shape, kind))
        extra = [half, right]
        scratch.append(pltpu.SemaphoreType.DMA((2,)))
    return pl.pallas_call(
        functools.partial(inner_kernel, sizes, len(parts)),
        in_specs=[SCALARS] + [WHOLE] * (1 + len(parts)) + [SCALARS, ANYWHERE][: len(extra)],
        out_specs=[WHOLE] * len(shape),
        out_shape=shape,
        scratch_shapes=scratch,
        compiler_params=params(),
        cost_estimate=COST,
    )(places, *held([rows, *parts]), *extra)


def products(inner_refs, right, outs, j):
    for e, ref in enumerate(inner_refs):
        value = lax.dot_general(
            ref[...], right, (((1,), (1,)), ((), ())), preferred_element_type=jnp.float32
        )
        at = 0
        for out_ref in outs:
            size = out_ref.shape[2]
            out_ref[j, e] = value[at : at + size, :].astype(out_ref.dtype)
            at += size


def own_kernel(n_inner, *refs):
    inner_refs, own_ref, outs = refs[:n_inner], refs[n_inner], refs[n_inner + 1 :]
    products(inner_refs, own_ref[0], outs[:PIECES], 0)
    products(inner_refs, own_ref[1], outs[PIECES:], 0)


def keep_kernel(n_inner, *refs):
    inner_refs, near_refs, outs = refs[:n_inner], refs[n_inner:-PIECES], refs[-PIECES:]
    for j, ref in enumerate(near_refs):
        products(inner_refs, ref[...], outs, j)


def outer_of(inners, own, gives, keeps, sizes):
    _, rows, depth = own.shape

    def shapes(blocks, kind):
        return [vmem((blocks, len(inners), size, rows), kind) for size in sizes]

    made = pl.pallas_call(
        functools.partial(own_kernel, len(inners)),
        in_specs=[WHOLE] * (len(inners) + 1),
        out_specs=[WHOLE] * (2 * PIECES),
        out_shape=shapes(1, jnp.bfloat16) + shapes(1, jnp.float32),
        compiler_params=params(),
        cost_estimate=COST,
    )(*held([*inners, own]))
    give, keep = [list(made[:PIECES])], [list(made[PIECES:])]
    for nears, kind, into in ((gives, jnp.bfloat16, give), (keeps, jnp.float32, keep)):
        made = pl.pallas_call(
            functools.partial(keep_kernel, len(inners)),
            in_specs=[WHOLE] * (len(inners) + len(nears)),
            out_specs=[WHOLE] * PIECES,
            out_shape=shapes(len(nears), kind),
            compiler_params=params(),
            cost_estimate=COST,
        )(*held([*inners, *after(nears, made)]))
        into.append(list(made))
    return give, keep


def cores_kernel(index_ref, *refs):
    (own_ref, near_ref), (got_own_ref, got_near_ref), (kept_ref, sent_ref) = refs[:2], refs[2:4], refs[4:]
    for k in range(index_ref.shape[0]):
        block = index_ref[k]
        for j in range(kept_ref.shape[0]):
            if j == 0:
                total = own_ref[0, block] + got_own_ref[0, block]
            else:
                total = near_ref[j - 1, block] + got_near_ref[j - 1, block]
            if k == 0:
                kept_ref[j] = total
            else:
                sent_ref[k - 1, j] = total.astype(sent_ref.dtype)


def cores_summed(keep, got, index):
    near, _, height, wide = keep[1].shape
    others = index.shape[0] - 1
    return pl.pallas_call(
        cores_kernel,
        in_specs=[SCALARS] + [WHOLE] * 4,
        out_specs=[WHOLE, WHOLE],
        out_shape=[
            vmem((1 + near, height, wide), jnp.float32),
            vmem((others, 1 + near, height, wide), jnp.bfloat16),
        ],
        compiler_params=params(),
        cost_estimate=COST,
    )(index, *held([*keep, *got]))


def chosen_kernel(index_ref, *refs):
    n = index_ref.shape[0]
    for k, out_ref in enumerate(refs[n:]):
        for j in range(out_ref.shape[0]):
            value = refs[0][j].astype(jnp.float32)
            for i in range(1, n):
                value = jnp.where(index_ref[k] == i, refs[i][j].astype(jnp.float32), value)
            out_ref[j] = value.astype(out_ref.dtype)


def chosen_of(values, index):
    kinds = [jnp.float32] + [jnp.bfloat16] * (len(values) - 1)
    return pl.pallas_call(
        chosen_kernel,
        in_specs=[SCALARS] + [WHOLE] * len(values),
        out_specs=[WHOLE] * len(values),
        out_shape=[vmem(values[0].shape, kind) for kind in kinds],
        compiler_params=params(),
        cost_estimate=COST,
    )(index, *held(values))


def planes_kernel(n_got, index_ref, kept_ref, *refs):
    got_refs = refs[:n_got]
    final_ref, sent_ref = refs[n_got:]
    for k in range(index_ref.shape[0]):
        block = index_ref[k]
        total = kept_ref[block]
        for ref in got_refs:
            total = total + ref[block].astype(jnp.float32)
        if k == 0:
            final_ref[...] = total
        else:
            sent_ref[k - 1] = total.astype(sent_ref.dtype)


def planes_summed(kept, got, index):
    blocks, height, wide = kept.shape
    return pl.pallas_call(
        functools.partial(planes_kernel, len(got)),
        in_specs=[SCALARS] + [WHOLE] * (1 + len(got)),
        out_specs=[WHOLE, WHOLE],
        out_shape=[
            vmem((height, wide), jnp.float32),
            vmem((blocks - 1, height, wide), jnp.bfloat16),
        ],
        compiler_params=params(),
        cost_estimate=COST,
    )(index, *held([kept, *got]))


def after(value, *earlier):
    return lax.optimization_barrier((value, *earlier))[0]


def shards(psi, left_ops, right_ops, block_mask):
    terms, n = lax.axis_size("term"), lax.axis_size("row")
    s = math.isqrt(n)
    assert s * s == n and terms == 2 * n and left_ops.shape[0] == 1
    height, width = psi.shape
    term, row = lax.axis_index("term"), lax.axis_index("row")
    core, z = term % 2, term // 2
    zh, zl = z // s, z % s
    hi, lo = row // s, row % s

    def from_lo(value, j):
        pairs = [(a * s + (b + j) % s, a * s + b) for a in range(s) for b in range(s)]
        return lax.ppermute(value, "row", pairs)

    def from_hi(value, j):
        pairs = [(((a + j) % s) * s + b, a * s + b) for a in range(s) for b in range(s)]
        return lax.ppermute(value, "row", pairs)

    def from_term(value, bit):
        return lax.ppermute(value, "term", [(a ^ bit, a) for a in range(terms)])

    def to_zl(value, j):
        pairs = [
            ((a * s + b) * 2 + c, (a * s + (b + j) % s) * 2 + c)
            for a in range(s) for b in range(s) for c in range(2)
        ]
        return lax.ppermute(value, "term", pairs)

    def to_zh(value, j):
        pairs = [
            ((a * s + b) * 2 + c, (((a + j) % s) * s + b) * 2 + c)
            for a in range(s) for b in range(s) for c in range(2)
        ]
        return lax.ppermute(value, "term", pairs)

    def crossed(value):
        pairs = [
            (((a * s + b) * 2 + c) * n + y * s + x, ((a * s + x) * 2 + c) * n + y * s + b)
            for a in range(s) for b in range(s) for c in range(2) for y in range(s) for x in range(s)
        ]
        return lax.ppermute(value, ("term", "row"), pairs)

    sharing = min(SHARE, max(1, height // 128))
    share = height // sharing
    mine = term % sharing
    own_share = share_of(psi, mine * share, share)
    depth = n * height

    near_x = [from_lo(own_share, j) for j in range(1, s)]
    near_y = [from_hi(own_share, j) for j in range(1, s)]
    own_share, term, row = lax.optimization_barrier((own_share, term, row))
    core, z, mine = term % 2, term // 2, term % sharing
    zh, zl, hi, lo = z // s, z % s, row // s, row % s

    def place(jy, jx, bits):
        return ((hi + jy) % s * s + (lo + jx) % s) * height + (mine ^ bits) * share

    def members(own, base):
        return jnp.stack([(own + j - base) % s for j in range(s)]).astype(jnp.int32)

    at_near = [(0, j) for j in range(1, s)] + [(j, 0) for j in range(1, s)]
    at_far = [(jy, jx) for jy in range(1, s) for jx in range(1, s)]
    held = [place(*at, bits) for bits in range(sharing) for at in at_near + at_far]
    sizes = [height] + [share] * len(held)
    places = jnp.stack([row * height] + held).astype(jnp.int32)
    half = (1 - core).astype(jnp.int32).reshape(1)
    counted = jnp.arange(s, dtype=jnp.int32)
    halves = right_ops[0].reshape(2, height // 2, width)
    own_give, own_keep = [lax.dynamic_index_in_dim(halves, k, 0, keepdims=False) for k in (1 - core, core)]
    near_x, near_y, own_left, own_give, own_keep, places, half, by_zl, by_zh, counted = lax.optimization_barrier(
        (near_x, near_y, masked_rows(left_ops[0], block_mask[0]), own_give, own_keep, places, half, members(zl, lo), members(zh, hi), counted)
    )
    far = [from_hi(v, jy) for jy in range(1, s) for v in near_x]
    near = jnp.concatenate(near_x + near_y, 0)
    far = stacked(far) if len(far) > 1 else far[0]
    first, last = [(at_near, 0, near), (at_far, 0, far)], []
    if sharing > 1:
        near_core = from_term(near, 1)
        first += [(at_near, 1, near_core), (at_far, 1, from_term(far, 1))]
    early = stacked([psi] + [v for _, _, v in first])
    gives = [from_hi(after(own_give, near), j) for j in range(1, s)]
    keeps = [from_hi(after(own_keep, gives), j) for j in range(1, s)]
    if sharing > 2:
        near_z, far_z = from_term(near, 2), from_term(far, 2)
        last = [(at_near, 2, near_z), (at_far, 2, far_z)]
        last += [(at_near, 3, from_term(after(near_z, (early, gives)), 1)), (at_far, 3, from_term(far_z, 1))]
    parts = [early] + [v for _, _, v in last]

    near_left = [from_lo(own_left, j) for j in range(1, s)]
    inners = list(inner_of(own_left, parts, sizes, places))
    for rows in near_left:
        rows = after(rows, inners[-1])
        inner, own_halves = inner_of(rows, parts, sizes, places, halves, half)
        inners.append(inner)

    cut = height * FIRST[0] // FIRST[1] // 32 * 32
    row_sizes = [cut, height - cut]
    give, keep = outer_of(inners, own_halves, gives, keeps, row_sizes)
    got = [[from_term(v, 1) for v in group] for group in give]
    outs = []
    for p in range(PIECES):
        home_first = p % 2 == 1
        index = counted if home_first else by_zl
        kept, sent = cores_summed([v[p] for v in keep], [v[p] for v in got], index)
        if home_first:
            held_blocks = [kept] + [from_lo(sent[s - j - 1], j) for j in range(1, s)]
            kept, *sent = chosen_of(held_blocks, by_zl)
        final, sent = planes_summed(kept, [to_zl(sent[j - 1], j) for j in range(1, s)], by_zh)
        for j in range(1, s):
            final = final + to_zh(sent[j - 1], j).astype(jnp.float32)
        final = final.astype(jnp.bfloat16)
        outs.append(final if home_first else crossed(final))
    return jnp.concatenate(outs, 0)


def solution(mesh):
    in_specs = (
        P("row", None),
        P("term", "row", None),
        P("term", "row", None),
        P("term", "row", None),
    )
    out_specs = P("row", "term")
    return jax.shard_map(shards, mesh=mesh, in_specs=in_specs, out_specs=out_specs, check_vma=False)
```

```python
import functools
import math

import jax
import jax.numpy as jnp
from jax import lax
from jax.experimental import pallas as pl
from jax.experimental.pallas import tpu as pltpu
from jax.sharding import PartitionSpec as P

SHARE = 4
PIECES = 2
FIRST = (9, 16)
VMEM_BYTES = 20 * 1024 * 1024
COST = pl.CostEstimate(flops=1, bytes_accessed=1, transcendentals=0)
WHOLE = pl.BlockSpec(memory_space=pltpu.VMEM)
SCALARS = pl.BlockSpec(memory_space=pltpu.SMEM)
ANYWHERE = pl.BlockSpec(memory_space=pl.ANY)


def vmem(shape, kind):
    return pltpu.VMEM(shape, kind)


def held(values):
    return [pltpu.with_memory_space_constraint(v, pltpu.VMEM) for v in values]


def params():
    return pltpu.CompilerParams(vmem_limit_bytes=VMEM_BYTES)


def mask_kernel(blk, mask_ref, left_ref, out_ref):
    for j in range(left_ref.shape[1] // blk):
        keep = mask_ref[pl.program_id(0), j] != 0
        cols = pl.ds(j * blk, blk)
        tile = left_ref[:, cols]
        out_ref[:, cols] = jnp.where(keep, tile, jnp.zeros_like(tile))


def masked_rows(left, mask):
    rows, width = left.shape
    blk = width // mask.shape[1]
    spec = pl.BlockSpec((blk, width), lambda i: (i, 0))
    return pl.pallas_call(
        functools.partial(mask_kernel, blk),
        grid=(rows // blk,),
        in_specs=[SCALARS, spec],
        out_specs=spec,
        out_shape=jax.ShapeDtypeStruct((rows, width), left.dtype),
        compiler_params=params(),
        cost_estimate=COST,
    )(mask, left)


def share_kernel(start_ref, whole_ref, out_ref, sem):
    size = out_ref.shape[0]
    where = pl.ds(pl.multiple_of(start_ref[0], size), size)
    copy = pltpu.make_async_copy(whole_ref.at[where], out_ref, sem)
    copy.start()
    copy.wait()


def share_of(whole, start, size):
    return pl.pallas_call(
        share_kernel,
        in_specs=[SCALARS, ANYWHERE],
        out_specs=WHOLE,
        out_shape=vmem((size, whole.shape[1]), whole.dtype),
        scratch_shapes=[pltpu.SemaphoreType.DMA],
        compiler_params=params(),
        cost_estimate=COST,
    )(start.astype(jnp.int32).reshape(1), pltpu.with_memory_space_constraint(whole, pltpu.HBM))


def stack_kernel(*refs):
    part_refs, (whole, sems) = refs[:-2], refs[-2:]
    copies, at = [], 0
    for p, part in enumerate(part_refs):
        size = part.shape[0]
        copies.append(pltpu.make_async_copy(part, whole.at[pl.ds(at, size)], sems.at[p]))
        at += size
    for copy in copies:
        copy.start()
    for copy in copies:
        copy.wait()


def stacked(parts):
    depth, width = sum(a.shape[0] for a in parts), parts[0].shape[1]
    return pl.pallas_call(
        stack_kernel,
        in_specs=[ANYWHERE] * len(parts),
        out_specs=ANYWHERE,
        out_shape=vmem((depth, width), parts[0].dtype),
        scratch_shapes=[pltpu.SemaphoreType.DMA((len(parts),))],
        compiler_params=params(),
        cost_estimate=COST,
    )(*parts)


def inner_kernel(sizes, n_parts, place_ref, rows_ref, *refs):
    part_refs, refs = refs[:n_parts], refs[n_parts:]
    copies = []
    if len(refs) > 2:
        half_ref, right_ref, out_ref, right_out, ordered, sems = refs
        for k in range(2):
            half = half_ref[0] if k == 0 else 1 - half_ref[0]
            copies.append(pltpu.make_async_copy(right_ref.at[half], right_out.at[k], sems.at[k]))
            copies[-1].start()
    else:
        out_ref, ordered = refs
    at = 0
    for p, size in enumerate(sizes):
        cols = pl.ds(pl.multiple_of(place_ref[p], size), size)
        ordered[:, at : at + size] = rows_ref[:, cols]
        at += size
    step = math.gcd(out_ref.shape[1], 512)
    for j in range(out_ref.shape[1] // step):
        cols = pl.ds(j * step, step)
        psi = jnp.concatenate([ref[:, cols] for ref in part_refs], 0)
        value = jnp.dot(ordered[...], psi, preferred_element_type=jnp.float32)
        out_ref[:, cols] = value.astype(out_ref.dtype)
    for copy in copies:
        copy.wait()


def inner_of(rows, parts, sizes, places, right=None, half=None):
    height, depth = rows.shape
    kind = parts[0].dtype
    shape, extra, scratch = [vmem((height, parts[0].shape[1]), kind)], [], [pltpu.VMEM((height, depth), kind)]
    if right is not None:
        shape.append(vmem(right.shape, kind))
        extra = [half, right]
        scratch.append(pltpu.SemaphoreType.DMA((2,)))
    return pl.pallas_call(
        functools.partial(inner_kernel, sizes, len(parts)),
        in_specs=[SCALARS] + [WHOLE] * (1 + len(parts)) + [SCALARS, ANYWHERE][: len(extra)],
        out_specs=[WHOLE] * len(shape),
        out_shape=shape,
        scratch_shapes=scratch,
        compiler_params=params(),
        cost_estimate=COST,
    )(places, *held([rows, *parts]), *extra)


def products(inner_refs, right, outs, j):
    for e, ref in enumerate(inner_refs):
        value = lax.dot_general(
            ref[...], right, (((1,), (1,)), ((), ())), preferred_element_type=jnp.float32
        )
        at = 0
        for out_ref in outs:
            size = out_ref.shape[2]
            out_ref[j, e] = value[at : at + size, :].astype(out_ref.dtype)
            at += size


def rows_kernel(n_give, inner_ref, own_ref, *refs):
    give_refs, outs = refs[:n_give], refs[n_give:]
    products([inner_ref], own_ref[0], outs[:PIECES], 0)
    products([inner_ref], own_ref[1], outs[PIECES:], 0)
    for j, ref in enumerate(give_refs):
        products([inner_ref], ref[...], outs[:PIECES], 1 + j)


def rows_of(inner, own, gives, sizes):
    cols = own.shape[1]
    give = [vmem((1 + len(gives), 1, size, cols), jnp.bfloat16) for size in sizes]
    keep = [vmem((1, 1, size, cols), jnp.float32) for size in sizes]
    made = pl.pallas_call(
        functools.partial(rows_kernel, len(gives)),
        in_specs=[WHOLE] * (2 + len(gives)),
        out_specs=[WHOLE] * (2 * PIECES),
        out_shape=give + keep,
        compiler_params=params(),
        cost_estimate=COST,
    )(*held([inner, own, *gives]))
    return list(made[:PIECES]), list(made[PIECES:])


def keep_kernel(n_inner, *refs):
    inner_refs, near_refs, outs = refs[:n_inner], refs[n_inner:-PIECES], refs[-PIECES:]
    for j, ref in enumerate(near_refs):
        products(inner_refs, ref[...], outs, j)


def keep_of(inners, nears, sizes):
    cols = nears[0].shape[0]
    made = pl.pallas_call(
        functools.partial(keep_kernel, len(inners)),
        in_specs=[WHOLE] * (len(inners) + len(nears)),
        out_specs=[WHOLE] * PIECES,
        out_shape=[vmem((len(nears), len(inners), size, cols), jnp.float32) for size in sizes],
        compiler_params=params(),
        cost_estimate=COST,
    )(*held([*inners, *nears]))
    return list(made)


def cores_kernel(index_ref, near_ref, *refs):
    n = (len(refs) - 2) // 2
    own_refs, got_refs, (kept_ref, sent_ref) = refs[:n], refs[n : 2 * n], refs[2 * n :]
    for k in range(n):
        for e in range(n):

            @pl.when(index_ref[k] == e)
            def _(k=k, e=e):
                for j in range(kept_ref.shape[0]):
                    mine = own_refs[e][0, 0] if j == 0 else near_ref[j - 1, e]
                    total = mine + got_refs[e][j, 0]
                    if k == 0:
                        kept_ref[j] = total
                    else:
                        sent_ref[k - 1, j] = total.astype(sent_ref.dtype)


def cores_summed(near, own, got, index):
    blocks, _, height, wide = near.shape
    others = index.shape[0] - 1
    return pl.pallas_call(
        cores_kernel,
        in_specs=[SCALARS] + [WHOLE] * (1 + len(own) + len(got)),
        out_specs=[WHOLE, WHOLE],
        out_shape=[
            vmem((1 + blocks, height, wide), jnp.float32),
            vmem((others, 1 + blocks, height, wide), jnp.bfloat16),
        ],
        compiler_params=params(),
        cost_estimate=COST,
    )(index, *held([near, *own, *got]))


def chosen_kernel(index_ref, *refs):
    n = index_ref.shape[0]
    for k, out_ref in enumerate(refs[n:]):
        for j in range(out_ref.shape[0]):
            value = refs[0][j].astype(jnp.float32)
            for i in range(1, n):
                value = jnp.where(index_ref[k] == i, refs[i][j].astype(jnp.float32), value)
            out_ref[j] = value.astype(out_ref.dtype)


def chosen_of(values, index):
    kinds = [jnp.float32] + [jnp.bfloat16] * (len(values) - 1)
    return pl.pallas_call(
        chosen_kernel,
        in_specs=[SCALARS] + [WHOLE] * len(values),
        out_specs=[WHOLE] * len(values),
        out_shape=[vmem(values[0].shape, kind) for kind in kinds],
        compiler_params=params(),
        cost_estimate=COST,
    )(index, *held(values))


def planes_kernel(n_got, index_ref, kept_ref, *refs):
    got_refs = refs[:n_got]
    final_ref, sent_ref = refs[n_got:]
    for k in range(index_ref.shape[0]):
        block = index_ref[k]
        total = kept_ref[block]
        for ref in got_refs:
            total = total + ref[block].astype(jnp.float32)
        if k == 0:
            final_ref[...] = total
        else:
            sent_ref[k - 1] = total.astype(sent_ref.dtype)


def planes_summed(kept, got, index):
    blocks, height, wide = kept.shape
    return pl.pallas_call(
        functools.partial(planes_kernel, len(got)),
        in_specs=[SCALARS] + [WHOLE] * (1 + len(got)),
        out_specs=[WHOLE, WHOLE],
        out_shape=[
            vmem((height, wide), jnp.float32),
            vmem((blocks - 1, height, wide), jnp.bfloat16),
        ],
        compiler_params=params(),
        cost_estimate=COST,
    )(index, *held([kept, *got]))


def after(value, *earlier):
    return lax.optimization_barrier((value, *earlier))[0]


def shards(psi, left_ops, right_ops, block_mask):
    terms, n = lax.axis_size("term"), lax.axis_size("row")
    s = math.isqrt(n)
    assert s * s == n and terms == 2 * n and left_ops.shape[0] == 1
    height, width = psi.shape
    term, row = lax.axis_index("term"), lax.axis_index("row")
    core, z = term % 2, term // 2
    zh, zl = z // s, z % s
    hi, lo = row // s, row % s

    def from_lo(value, j):
        pairs = [(a * s + (b + j) % s, a * s + b) for a in range(s) for b in range(s)]
        return lax.ppermute(value, "row", pairs)

    def from_hi(value, j):
        pairs = [(((a + j) % s) * s + b, a * s + b) for a in range(s) for b in range(s)]
        return lax.ppermute(value, "row", pairs)

    def from_term(value, bit):
        return lax.ppermute(value, "term", [(a ^ bit, a) for a in range(terms)])

    def to_zl(value, j):
        pairs = [
            ((a * s + b) * 2 + c, (a * s + (b + j) % s) * 2 + c)
            for a in range(s) for b in range(s) for c in range(2)
        ]
        return lax.ppermute(value, "term", pairs)

    def to_zh(value, j):
        pairs = [
            ((a * s + b) * 2 + c, (((a + j) % s) * s + b) * 2 + c)
            for a in range(s) for b in range(s) for c in range(2)
        ]
        return lax.ppermute(value, "term", pairs)

    def crossed(value):
        pairs = [
            (((a * s + b) * 2 + c) * n + y * s + x, ((a * s + x) * 2 + c) * n + y * s + b)
            for a in range(s) for b in range(s) for c in range(2) for y in range(s) for x in range(s)
        ]
        return lax.ppermute(value, ("term", "row"), pairs)

    sharing = min(SHARE, max(1, height // 128))
    share = height // sharing
    mine = term % sharing
    own_share = share_of(psi, mine * share, share)
    depth = n * height

    near_x = [from_lo(own_share, j) for j in range(1, s)]
    near_y = [from_hi(own_share, j) for j in range(1, s)]
    own_share, term, row = lax.optimization_barrier((own_share, term, row))
    core, z, mine = term % 2, term // 2, term % sharing
    zh, zl, hi, lo = z // s, z % s, row // s, row % s

    def place(jy, jx, bits):
        return ((hi + jy) % s * s + (lo + jx) % s) * height + (mine ^ bits) * share

    def members(own, base):
        return jnp.stack([(own + j - base) % s for j in range(s)]).astype(jnp.int32)

    at_near = [(0, j) for j in range(1, s)] + [(j, 0) for j in range(1, s)]
    at_far = [(jy, jx) for jy in range(1, s) for jx in range(1, s)]
    held = [place(*at, bits) for bits in range(sharing) for at in at_near + at_far]
    sizes = [height] + [share] * len(held)
    places = jnp.stack([row * height] + held).astype(jnp.int32)
    half = (1 - core).astype(jnp.int32).reshape(1)
    counted = jnp.arange(s, dtype=jnp.int32)
    halves = right_ops[0].reshape(2, height // 2, width)
    own_give, own_keep = [lax.dynamic_index_in_dim(halves, k, 0, keepdims=False) for k in (1 - core, core)]
    near_x, near_y, own_left, own_give, own_keep, places, half, by_zl, by_zh, counted = lax.optimization_barrier(
        (near_x, near_y, masked_rows(left_ops[0], block_mask[0]), own_give, own_keep, places, half, members(zl, lo), members(zh, hi), counted)
    )
    far = [from_hi(v, jy) for jy in range(1, s) for v in near_x]
    near = jnp.concatenate(near_x + near_y, 0)
    far = stacked(far) if len(far) > 1 else far[0]
    first, last = [(at_near, 0, near), (at_far, 0, far)], []
    if sharing > 1:
        near_core = from_term(near, 1)
        first += [(at_near, 1, near_core), (at_far, 1, from_term(far, 1))]
    early = stacked([psi] + [v for _, _, v in first])
    gives = [from_hi(after(own_give, near), j) for j in range(1, s)]
    keeps = [from_hi(after(own_keep, gives), j) for j in range(1, s)]
    if sharing > 2:
        near_z, far_z = from_term(near, 2), from_term(far, 2)
        last = [(at_near, 2, near_z), (at_far, 2, far_z)]
        last += [(at_near, 3, from_term(after(near_z, (early, gives)), 1)), (at_far, 3, from_term(far_z, 1))]
    parts = [early] + [v for _, _, v in last]

    near_left = [from_lo(own_left, j) for j in range(1, s)]
    cut = height * FIRST[0] // FIRST[1] // 32 * 32
    row_sizes = [cut, height - cut]
    inner, own_halves = inner_of(own_left, parts, sizes, places, halves, half)
    inners, own, got = [inner], [], []
    for rows in [*near_left, None]:
        give, keep = rows_of(inners[-1], own_halves, gives, row_sizes)
        own.append(keep)
        got.append([from_term(v, 1) for v in give])
        if rows is not None:
            inners += inner_of(after(rows, keep), parts, sizes, places)
    near_keep = keep_of(inners, after(keeps, own), row_sizes)
    outs = []
    for p in range(PIECES):
        home_first = p % 2 == 1
        index = counted if home_first else by_zl
        kept, sent = cores_summed(near_keep[p], [v[p] for v in own], [v[p] for v in got], index)
        if home_first:
            held_blocks = [kept] + [from_lo(sent[s - j - 1], j) for j in range(1, s)]
            kept, *sent = chosen_of(held_blocks, by_zl)
        final, sent = planes_summed(kept, [to_zl(sent[j - 1], j) for j in range(1, s)], by_zh)
        for j in range(1, s):
            final = final + to_zh(sent[j - 1], j).astype(jnp.float32)
        final = final.astype(jnp.bfloat16)
        outs.append(final if home_first else crossed(final))
    return jnp.concatenate(outs, 0)


def solution(mesh):
    in_specs = (
        P("row", None),
        P("term", "row", None),
        P("term", "row", None),
        P("term", "row", None),
    )
    out_specs = P("row", "term")
    return jax.shard_map(shards, mesh=mesh, in_specs=in_specs, out_specs=out_specs, check_vma=False)
```

```python
import functools
import math

import jax
import jax.numpy as jnp
from jax import lax
from jax.experimental import pallas as pl
from jax.experimental.pallas import tpu as pltpu
from jax.sharding import PartitionSpec as P

SHARE = 4
PIECES = 2
FIRST = (1, 2)
VMEM_BYTES = 20 * 1024 * 1024
COST = pl.CostEstimate(flops=1, bytes_accessed=1, transcendentals=0)
WHOLE = pl.BlockSpec(memory_space=pltpu.VMEM)
SCALARS = pl.BlockSpec(memory_space=pltpu.SMEM)
ANYWHERE = pl.BlockSpec(memory_space=pl.ANY)


def vmem(shape, kind):
    return pltpu.VMEM(shape, kind)


def held(values):
    return [pltpu.with_memory_space_constraint(v, pltpu.VMEM) for v in values]


def params():
    return pltpu.CompilerParams(vmem_limit_bytes=VMEM_BYTES)


def mask_kernel(blk, mask_ref, left_ref, out_ref):
    for j in range(left_ref.shape[1] // blk):
        keep = mask_ref[pl.program_id(0), j] != 0
        cols = pl.ds(j * blk, blk)
        tile = left_ref[:, cols]
        out_ref[:, cols] = jnp.where(keep, tile, jnp.zeros_like(tile))


def masked_rows(left, mask):
    rows, width = left.shape
    blk = width // mask.shape[1]
    spec = pl.BlockSpec((blk, width), lambda i: (i, 0))
    return pl.pallas_call(
        functools.partial(mask_kernel, blk),
        grid=(rows // blk,),
        in_specs=[SCALARS, spec],
        out_specs=spec,
        out_shape=jax.ShapeDtypeStruct((rows, width), left.dtype),
        compiler_params=params(),
        cost_estimate=COST,
    )(mask, left)


def share_kernel(start_ref, whole_ref, out_ref, sem):
    size = out_ref.shape[0]
    where = pl.ds(pl.multiple_of(start_ref[0], size), size)
    copy = pltpu.make_async_copy(whole_ref.at[where], out_ref, sem)
    copy.start()
    copy.wait()


def share_of(whole, start, size):
    return pl.pallas_call(
        share_kernel,
        in_specs=[SCALARS, ANYWHERE],
        out_specs=WHOLE,
        out_shape=vmem((size, whole.shape[1]), whole.dtype),
        scratch_shapes=[pltpu.SemaphoreType.DMA],
        compiler_params=params(),
        cost_estimate=COST,
    )(start.astype(jnp.int32).reshape(1), pltpu.with_memory_space_constraint(whole, pltpu.HBM))


def stack_kernel(*refs):
    part_refs, (whole, sems) = refs[:-2], refs[-2:]
    copies, at = [], 0
    for p, part in enumerate(part_refs):
        size = part.shape[0]
        copies.append(pltpu.make_async_copy(part, whole.at[pl.ds(at, size)], sems.at[p]))
        at += size
    for copy in copies:
        copy.start()
    for copy in copies:
        copy.wait()


def stacked(parts):
    depth, width = sum(a.shape[0] for a in parts), parts[0].shape[1]
    return pl.pallas_call(
        stack_kernel,
        in_specs=[ANYWHERE] * len(parts),
        out_specs=ANYWHERE,
        out_shape=vmem((depth, width), parts[0].dtype),
        scratch_shapes=[pltpu.SemaphoreType.DMA((len(parts),))],
        compiler_params=params(),
        cost_estimate=COST,
    )(*parts)


def inner_kernel(sizes, n_parts, place_ref, rows_ref, *refs):
    part_refs, refs = refs[:n_parts], refs[n_parts:]
    copies = []
    if len(refs) > 2:
        half_ref, right_ref, out_ref, right_out, ordered, sems = refs
        for k in range(2):
            half = half_ref[0] if k == 0 else 1 - half_ref[0]
            copies.append(pltpu.make_async_copy(right_ref.at[half], right_out.at[k], sems.at[k]))
            copies[-1].start()
    else:
        out_ref, ordered = refs
    at = 0
    for p, size in enumerate(sizes):
        cols = pl.ds(pl.multiple_of(place_ref[p], size), size)
        ordered[:, at : at + size] = rows_ref[:, cols]
        at += size
    step = math.gcd(out_ref.shape[1], 512)
    for j in range(out_ref.shape[1] // step):
        cols = pl.ds(j * step, step)
        psi = jnp.concatenate([ref[:, cols] for ref in part_refs], 0)
        value = jnp.dot(ordered[...], psi, preferred_element_type=jnp.float32)
        out_ref[:, cols] = value.astype(out_ref.dtype)
    for copy in copies:
        copy.wait()


def inner_of(rows, parts, sizes, places, right=None, half=None):
    height, depth = rows.shape
    kind = parts[0].dtype
    shape, extra, scratch = [vmem((height, parts[0].shape[1]), kind)], [], [pltpu.VMEM((height, depth), kind)]
    if right is not None:
        shape.append(vmem(right.shape, kind))
        extra = [half, right]
        scratch.append(pltpu.SemaphoreType.DMA((2,)))
    return pl.pallas_call(
        functools.partial(inner_kernel, sizes, len(parts)),
        in_specs=[SCALARS] + [WHOLE] * (1 + len(parts)) + [SCALARS, ANYWHERE][: len(extra)],
        out_specs=[WHOLE] * len(shape),
        out_shape=shape,
        scratch_shapes=scratch,
        compiler_params=params(),
        cost_estimate=COST,
    )(places, *held([rows, *parts]), *extra)


def products(inner_refs, right, outs, j):
    for e, ref in enumerate(inner_refs):
        value = lax.dot_general(
            ref[...], right, (((1,), (1,)), ((), ())), preferred_element_type=jnp.float32
        )
        at = 0
        for out_ref in outs:
            size = out_ref.shape[2]
            out_ref[j, e] = value[at : at + size, :].astype(out_ref.dtype)
            at += size


def rows_kernel(n_give, inner_ref, own_ref, *refs):
    give_refs, outs = refs[:n_give], refs[n_give:]
    products([inner_ref], own_ref[0], outs[:PIECES], 0)
    products([inner_ref], own_ref[1], outs[PIECES:], 0)
    for j, ref in enumerate(give_refs):
        products([inner_ref], ref[...], outs[:PIECES], 1 + j)


def rows_of(inner, own, gives, sizes):
    cols = own.shape[1]
    give = [vmem((1 + len(gives), 1, size, cols), jnp.bfloat16) for size in sizes]
    keep = [vmem((1, 1, size, cols), jnp.float32) for size in sizes]
    made = pl.pallas_call(
        functools.partial(rows_kernel, len(gives)),
        in_specs=[WHOLE] * (2 + len(gives)),
        out_specs=[WHOLE] * (2 * PIECES),
        out_shape=give + keep,
        compiler_params=params(),
        cost_estimate=COST,
    )(*held([inner, own, *gives]))
    return list(made[:PIECES]), list(made[PIECES:])


def keep_kernel(n_inner, *refs):
    inner_refs, near_refs, outs = refs[:n_inner], refs[n_inner:-PIECES], refs[-PIECES:]
    for j, ref in enumerate(near_refs):
        products(inner_refs, ref[...], outs, j)


def keep_of(inners, nears, sizes):
    cols = nears[0].shape[0]
    made = pl.pallas_call(
        functools.partial(keep_kernel, len(inners)),
        in_specs=[WHOLE] * (len(inners) + len(nears)),
        out_specs=[WHOLE] * PIECES,
        out_shape=[vmem((len(nears), len(inners), size, cols), jnp.float32) for size in sizes],
        compiler_params=params(),
        cost_estimate=COST,
    )(*held([*inners, *nears]))
    return list(made)


def cores_kernel(index_ref, near_ref, *refs):
    n = (len(refs) - 2) // 2
    own_refs, got_refs, (kept_ref, sent_ref) = refs[:n], refs[n : 2 * n], refs[2 * n :]
    for k in range(n):
        for e in range(n):

            @pl.when(index_ref[k] == e)
            def _(k=k, e=e):
                for j in range(kept_ref.shape[0]):
                    mine = own_refs[e][0, 0] if j == 0 else near_ref[j - 1, e]
                    total = mine + got_refs[e][j, 0]
                    if k == 0:
                        kept_ref[j] = total
                    else:
                        sent_ref[k - 1, j] = total.astype(sent_ref.dtype)


def cores_summed(near, own, got, index):
    blocks, _, height, wide = near.shape
    others = index.shape[0] - 1
    return pl.pallas_call(
        cores_kernel,
        in_specs=[SCALARS] + [WHOLE] * (1 + len(own) + len(got)),
        out_specs=[WHOLE, WHOLE],
        out_shape=[
            vmem((1 + blocks, height, wide), jnp.float32),
            vmem((others, 1 + blocks, height, wide), jnp.bfloat16),
        ],
        compiler_params=params(),
        cost_estimate=COST,
    )(index, *held([near, *own, *got]))


def chosen_kernel(index_ref, *refs):
    n = index_ref.shape[0]
    for k, out_ref in enumerate(refs[n:]):
        for j in range(out_ref.shape[0]):
            value = refs[0][j].astype(jnp.float32)
            for i in range(1, n):
                value = jnp.where(index_ref[k] == i, refs[i][j].astype(jnp.float32), value)
            out_ref[j] = value.astype(out_ref.dtype)


def chosen_of(values, index):
    kinds = [jnp.float32] + [jnp.bfloat16] * (len(values) - 1)
    return pl.pallas_call(
        chosen_kernel,
        in_specs=[SCALARS] + [WHOLE] * len(values),
        out_specs=[WHOLE] * len(values),
        out_shape=[vmem(values[0].shape, kind) for kind in kinds],
        compiler_params=params(),
        cost_estimate=COST,
    )(index, *held(values))


def planes_kernel(n_got, index_ref, kept_ref, *refs):
    got_refs = refs[:n_got]
    final_ref, sent_ref = refs[n_got:]
    for k in range(index_ref.shape[0]):
        block = index_ref[k]
        total = kept_ref[block]
        for ref in got_refs:
            total = total + ref[block].astype(jnp.float32)
        if k == 0:
            final_ref[...] = total
        else:
            sent_ref[k - 1] = total.astype(sent_ref.dtype)


def planes_summed(kept, got, index):
    blocks, height, wide = kept.shape
    return pl.pallas_call(
        functools.partial(planes_kernel, len(got)),
        in_specs=[SCALARS] + [WHOLE] * (1 + len(got)),
        out_specs=[WHOLE, WHOLE],
        out_shape=[
            vmem((height, wide), jnp.float32),
            vmem((blocks - 1, height, wide), jnp.bfloat16),
        ],
        compiler_params=params(),
        cost_estimate=COST,
    )(index, *held([kept, *got]))


def after(value, *earlier):
    return lax.optimization_barrier((value, *earlier))[0]


def shards(psi, left_ops, right_ops, block_mask):
    terms, n = lax.axis_size("term"), lax.axis_size("row")
    s = math.isqrt(n)
    assert s * s == n and terms == 2 * n and left_ops.shape[0] == 1
    height, width = psi.shape
    term, row = lax.axis_index("term"), lax.axis_index("row")
    core, z = term % 2, term // 2
    zh, zl = z // s, z % s
    hi, lo = row // s, row % s

    def from_lo(value, j):
        pairs = [(a * s + (b + j) % s, a * s + b) for a in range(s) for b in range(s)]
        return lax.ppermute(value, "row", pairs)

    def from_hi(value, j):
        pairs = [(((a + j) % s) * s + b, a * s + b) for a in range(s) for b in range(s)]
        return lax.ppermute(value, "row", pairs)

    def from_term(value, bit):
        return lax.ppermute(value, "term", [(a ^ bit, a) for a in range(terms)])

    def to_zl(value, j):
        pairs = [
            ((a * s + b) * 2 + c, (a * s + (b + j) % s) * 2 + c)
            for a in range(s) for b in range(s) for c in range(2)
        ]
        return lax.ppermute(value, "term", pairs)

    def to_zh(value, j):
        pairs = [
            ((a * s + b) * 2 + c, (((a + j) % s) * s + b) * 2 + c)
            for a in range(s) for b in range(s) for c in range(2)
        ]
        return lax.ppermute(value, "term", pairs)

    def crossed(value):
        pairs = [
            (((a * s + b) * 2 + c) * n + y * s + x, ((a * s + x) * 2 + c) * n + y * s + b)
            for a in range(s) for b in range(s) for c in range(2) for y in range(s) for x in range(s)
        ]
        return lax.ppermute(value, ("term", "row"), pairs)

    sharing = min(SHARE, max(1, height // 128))
    share = height // sharing
    mine = term % sharing
    own_share = share_of(psi, mine * share, share)
    depth = n * height

    near_x = [from_lo(own_share, j) for j in range(1, s)]
    near_y = [from_hi(own_share, j) for j in range(1, s)]
    own_share, term, row = lax.optimization_barrier((own_share, term, row))
    core, z, mine = term % 2, term // 2, term % sharing
    zh, zl, hi, lo = z // s, z % s, row // s, row % s

    def place(jy, jx, bits):
        return ((hi + jy) % s * s + (lo + jx) % s) * height + (mine ^ bits) * share

    def members(own, base):
        return jnp.stack([(own + j - base) % s for j in range(s)]).astype(jnp.int32)

    at_near = [(0, j) for j in range(1, s)] + [(j, 0) for j in range(1, s)]
    at_far = [(jy, jx) for jy in range(1, s) for jx in range(1, s)]
    held = [place(*at, bits) for bits in range(sharing) for at in at_near + at_far]
    sizes = [height] + [share] * len(held)
    places = jnp.stack([row * height] + held).astype(jnp.int32)
    half = (1 - core).astype(jnp.int32).reshape(1)
    counted = jnp.arange(s, dtype=jnp.int32)
    halves = right_ops[0].reshape(2, height // 2, width)
    own_give, own_keep = [lax.dynamic_index_in_dim(halves, k, 0, keepdims=False) for k in (1 - core, core)]
    near_x, near_y, own_left, own_give, own_keep, places, half, by_zl, by_zh, counted = lax.optimization_barrier(
        (near_x, near_y, masked_rows(left_ops[0], block_mask[0]), own_give, own_keep, places, half, members(zl, lo), members(zh, hi), counted)
    )
    far = [from_hi(v, jy) for jy in range(1, s) for v in near_x]
    near = jnp.concatenate(near_x + near_y, 0)
    far = stacked(far) if len(far) > 1 else far[0]
    first, last = [(at_near, 0, near), (at_far, 0, far)], []
    if sharing > 1:
        near_core = from_term(near, 1)
        first += [(at_near, 1, near_core), (at_far, 1, from_term(far, 1))]
    early = stacked([psi] + [v for _, _, v in first])
    gives = [from_hi(after(own_give, near), j) for j in range(1, s)]
    keeps = [from_hi(after(own_keep, gives), j) for j in range(1, s)]
    if sharing > 2:
        near_z, far_z = from_term(near, 2), from_term(far, 2)
        last = [(at_near, 2, near_z), (at_far, 2, far_z)]
        last += [(at_near, 3, from_term(after(near_z, (early, gives)), 1)), (at_far, 3, from_term(far_z, 1))]
    parts = [early] + [v for _, _, v in last]

    near_left = [from_lo(own_left, j) for j in range(1, s)]
    cut = height * FIRST[0] // FIRST[1] // 32 * 32
    row_sizes = [cut, height - cut]
    inner, own_halves = inner_of(own_left, parts, sizes, places, halves, half)
    inners, own, got = [inner], [], []
    for rows in [*near_left, None]:
        give, keep = rows_of(inners[-1], own_halves, gives, row_sizes)
        own.append(keep)
        got.append([from_term(v, 1) for v in give])
        if rows is not None:
            inners += inner_of(after(rows, keep), parts, sizes, places)
    near_keep = keep_of(inners, after(keeps, own), row_sizes)
    outs = []
    for p in range(PIECES):
        home_first = p % 2 == 1
        index = counted if home_first else by_zl
        kept, sent = cores_summed(near_keep[p], [v[p] for v in own], [v[p] for v in got], index)
        if home_first:
            held_blocks = [kept] + [from_lo(sent[s - j - 1], j) for j in range(1, s)]
            kept, *sent = chosen_of(held_blocks, by_zl)
        final, sent = planes_summed(kept, [to_zl(sent[j - 1], j) for j in range(1, s)], by_zh)
        for j in range(1, s):
            final = final + to_zh(sent[j - 1], j).astype(jnp.float32)
        final = final.astype(jnp.bfloat16)
        outs.append(final if home_first else crossed(final))
    return jnp.concatenate(outs, 0)


def solution(mesh):
    in_specs = (
        P("row", None),
        P("term", "row", None),
        P("term", "row", None),
        P("term", "row", None),
    )
    out_specs = P("row", "term")
    return jax.shard_map(shards, mesh=mesh, in_specs=in_specs, out_specs=out_specs, check_vma=False)
```
